128 devices in a mesh: grp: 16 (over y, x), tp: 8 (over z, core).
Axes of the slice: x: 4, y: 4, z: 4, core: 2. Of those that a mesh axis runs over, the one named last changes fastest.
Arguments:
- attn_out: bfloat16 [16384, 4096], P('grp', 'tp'), may hold values from -6 to 6
- o_proj: bfloat16 [4096, 8192], P(None, 'tp'), may hold values from -0.09375 to 0.09375
- residual: bfloat16 [16384, 8192], P('grp', 'tp'), may hold values from -80 to 80
- norm_gain: float32 [8192], P('tp'), may hold values from 0.5 to 1.5
- dest_group: int32 [16384, 1], P('grp'), may hold values from 0 to 15; in each aligned block of 1024 rows (0 to 1023, 1024 to 2047, ...) at most 128 rows name the same one
- accept_count: int32 [2048], P('grp'), may hold values from 1 to 8
- target_values: bfloat16 [16384, 512], P('grp'), may hold values from -6 to 6
- master: float32 [512, 8192], P('grp', 'tp'), may hold values from -0.0625 to 0.0625
- moment_one: float32 [512, 8192], P('grp', 'tp'), may hold values from -6 to 6
- moment_two: float32 [512, 8192], P('grp', 'tp'), may hold values from 0.25 to 4
Outputs:
- predictions: bfloat16 [32768, 512], P(('grp', 'tp'))
- new_master: float32 [512, 8192], P('grp', 'tp')
- new_moment_one: float32 [512, 8192], P('grp', 'tp')
- new_moment_two: float32 [512, 8192], P('grp', 'tp')
The draws below stay inside these ranges and needn't reach their ends.
Inputs may be any that keep to these rules, and one draw needn't show every extreme that they name: `dest_group`: within the rows of one group no drafter shard is named by more than 128 rows, a bound that some block reaches.
All inputs are finite; a program needn't handle non-finite values.
Results may differ from the reference program's by a relative error of at most 0.0057.
Values may be sent and summed in bfloat16 or wider, within the bound.
A program may use at most 128 MiB of HBM per device.

```python
import math
import jax
import jax.numpy as jnp
import numpy as np
from jax import lax

D = 8192
ATT = 4096
KVW = 512
SPEC = 8
R_GRP = 1024
REQS = 2048
TOKENS = 16384
CAP = 128
SLOTS = 2048
PRED_ROWS = 32768
N_GRP = 16


def draw_residual(key, part):
    key = jax.random.fold_in(key, 11)
    key_base, key_rows, key_cols = jax.random.split(key, 3)
    column = jnp.arange(D, dtype=jnp.float32) / D
    col_power = 0.5 * column + 0.5 * jax.random.uniform(key_cols, (D,), jnp.float32)
    row_power = jax.random.uniform(key_rows, (TOKENS, 1), jnp.float32)
    base = jnp.clip(jax.random.normal(key_base, (TOKENS, D), jnp.float32), -6.0, 6.0)
    values = base * 10.0 ** row_power * 10.0 ** col_power[None, :] * 0.1
    return values.astype(jnp.bfloat16)


def set_ends(array, rng, low, high):
    shape = array.shape
    spot = [jax.random.randint(jax.random.fold_in(rng, axis), (), 0, shape[axis]) for axis in range(len(shape))]
    array = array.at[tuple(spot)].set(low)
    longest = shape.index(max(shape))
    spot[longest] = (spot[longest] + 1) % shape[longest]
    return array.at[tuple(spot)].set(high)


def shard_levels(rng, dims, cuts, low, top_value):
    gain = 1.0
    for axis_at, shards_of in cuts:
        steps = jax.random.uniform(jax.random.fold_in(jax.random.fold_in(rng, 6), axis_at), (shards_of,), jnp.float32, low / len(cuts), top_value / len(cuts))
        gain = gain * jnp.repeat(jnp.exp(steps), dims[axis_at] // shards_of).reshape((-1,) + (1,) * (len(dims) - 1 - axis_at))
    return gain


def assign_block(stream_key, own, number, rows, number_of, top, bound, lean):
    order = jax.random.permutation(stream_key, number_of)
    heavy_load, usual = portions_of(number_of, rows * top, bound, lean, True), portions_of(number_of, rows * top, bound, lean, False)
    places = jnp.arange(number_of)

    def named(lengths, turn):
        used = int((lengths > 0).sum())
        fixed = max(1, used // 4)
        passed = fixed + (places - fixed + turn * (used - fixed)) % max(1, number_of - fixed)
        return jnp.zeros((number_of,), jnp.int32).at[order[jnp.where(places < fixed, places, passed)]].set(jnp.asarray(lengths, jnp.int32))

    lengths = jnp.where(number % 4 == 0, named(heavy_load, number // 4), named(usual, number - number // 4 - 1))
    mixed = jax.random.permutation(jax.random.fold_in(own, 3), number_of)
    giver, sink = mixed[0:number_of // 2 * 2:2], mixed[1:number_of // 2 * 2:2]
    margin = jnp.minimum(lengths[giver] - 1, bound - lengths[sink]) // 2
    margin = jnp.where((giver == order[0]) | (sink == order[0]) | (lengths[sink] == 0), 0, jnp.maximum(margin, 0))
    passed = jax.random.randint(jax.random.fold_in(own, 4), (number_of // 2,), 0, 1 << 20) % (margin + 1)
    lengths = lengths.at[giver].add(-passed).at[sink].add(passed)
    members = jnp.searchsorted(jnp.cumsum(lengths), jnp.arange(rows * top), side="right").astype(jnp.int32)
    table = members.reshape(top, rows).T
    table = table[jax.random.permutation(jax.random.fold_in(own, 1), rows)]
    turn = jax.random.randint(jax.random.fold_in(own, 2), (rows, 1), 0, top)
    return jnp.take_along_axis(table, (jnp.arange(top)[None, :] + turn) % top, axis=1)


def portions_of(amount, total, most, lean, full):
    weights = [(1 << 20) // math.isqrt(standing ** lean) + 1 for standing in range(1, amount + 1)]
    largest = most if full else min(most, max(-(-total // amount), total * weights[0] // sum(weights)))
    least = 1 if total - largest >= amount - 1 else 0
    counts, surplus = [largest] + [least] * (amount - 1), total - largest - least * (amount - 1)
    while surplus > 0:
        candidates = [i for i in range(1, amount) if counts[i] < largest] or [i for i in range(1, amount) if counts[i] < most]
        pool, remaining = sum([weights[i] for i in candidates]), surplus
        for i in candidates:
            extra = min(most - counts[i], max(1, remaining * weights[i] // pool), surplus)
            counts[i] = counts[i] + extra
            surplus = surplus - extra
    return np.array(counts)


def bell_draw(key, dims, scale, most, pieces=(), held_as=jnp.bfloat16):
    entries = jax.random.normal(key, dims, jnp.float32) * scale
    if len(pieces) > 0:
        entries = shard_levels(key, dims, pieces, -0.22, 0.18) * entries
    return jnp.clip(entries, min=-most, max=most).astype(held_as)


def setup_inputs(seed: int = 0) -> dict:
    key_of = jax.random.split(jax.random.key(seed), 11)
    attn_out = bell_draw(key_of[0], (TOKENS, ATT), 1.0, 6.0, ((0, 16), (1, 8)))
    o_proj = bell_draw(key_of[1], (ATT, D), ATT ** -0.5, 0.09375, ((1, 8),))
    residual = draw_residual(jax.random.fold_in(key_of[10], 71), 0)
    norm_gain = jnp.clip(1.0 + 0.1 * jax.random.normal(key_of[3], (D,), jnp.float32), 0.5, 1.5)
    dest_group_keys = jax.random.split(jax.random.fold_in(key_of[4], 1), TOKENS // R_GRP)
    dest_group_turns = jax.random.permutation(jax.random.fold_in(key_of[4], 3), TOKENS // R_GRP)
    dest_group = jax.vmap(lambda own, number: assign_block(jax.random.fold_in(key_of[4], 2), own, number, R_GRP, N_GRP, 1, CAP, 2))(dest_group_keys, dest_group_turns).reshape((TOKENS, 1))
    accept_count = set_ends(jax.random.randint(key_of[5], (REQS,), 1, SPEC + 1), jax.random.fold_in(key_of[5], 1), 1, SPEC).astype(jnp.int32)
    target_values = bell_draw(key_of[6], (TOKENS, KVW), 1.0, 6.0, ((0, 16),))
    master = bell_draw(key_of[7], (KVW, D), D ** -0.5, 0.0625, ((0, 16), (1, 8)), jnp.float32)
    moment_one = bell_draw(key_of[8], (KVW, D), 1.0, 6.0, ((0, 16), (1, 8)), jnp.float32)
    moment_two = jnp.clip(jnp.exp(math.log(4.0) - 2.7725887 * jax.random.uniform(key_of[9], (KVW, D), jnp.float32) ** shard_levels(key_of[9], (KVW, D), ((0, 16), (1, 8)), -0.2, 0.2)), 0.25, 4.0)
    return dict(attn_out=attn_out, o_proj=o_proj, residual=residual, norm_gain=norm_gain, dest_group=dest_group, accept_count=accept_count, target_values=target_values, master=master, moment_one=moment_one, moment_two=moment_two)


norm_eps = 1e-06
beta_one = 0.9
beta_two = 0.95
adam_eps = 1e-08
learn_rate = 0.01
decay_rate = 0.1
step_count = 10

def reference(attn_out, o_proj, residual, norm_gain, dest_group, accept_count, target_values, master, moment_one, moment_two):
    hidden = residual.astype(jnp.float32) + jnp.dot(attn_out, o_proj, preferred_element_type=jnp.float32)
    mean_square = lax.optimization_barrier(jnp.sum(hidden * hidden, axis=1, keepdims=True)) / D
    feature = (hidden * lax.rsqrt(mean_square + norm_eps) * norm_gain.astype(jnp.float32)[None, :]).astype(jnp.bfloat16)
    target_group = dest_group[:, 0]
    onehot = (target_group[:, None] == jnp.arange(N_GRP, dtype=jnp.int32)[None, :]).astype(jnp.int32)
    blocked = onehot.reshape(N_GRP, R_GRP, N_GRP)
    earlier = jnp.cumsum(blocked, axis=1) - blocked
    ranking = lax.optimization_barrier(jnp.sum(earlier * blocked, axis=2)).reshape(TOKENS)
    source = jnp.arange(TOKENS, dtype=jnp.int32) // R_GRP
    position = (target_group * SLOTS + source * CAP + ranking).astype(jnp.int32)
    live = (jnp.arange(TOKENS, dtype=jnp.int32) % SPEC < jnp.repeat(accept_count, SPEC)).astype(jnp.float32)
    slot_features = jnp.zeros((PRED_ROWS, D), jnp.bfloat16).at[position].set(feature)
    slot_targets = jnp.zeros((PRED_ROWS, KVW), jnp.bfloat16).at[position].set(target_values)
    slot_live = jnp.zeros((PRED_ROWS,), jnp.float32).at[position].set(live)
    values = jnp.dot(slot_features, master.astype(jnp.bfloat16).T, preferred_element_type=jnp.float32)
    predictions = values.astype(jnp.bfloat16)
    errors = (slot_live[:, None] * (values - slot_targets.astype(jnp.float32))).astype(jnp.bfloat16)
    gradient = jnp.dot(errors.T, slot_features, preferred_element_type=jnp.float32) / math.sqrt(TOKENS)
    first_moment = beta_one * moment_one + (1.0 - beta_one) * gradient
    second_moment = beta_two * moment_two + (1.0 - beta_two) * gradient * gradient
    update = first_moment / (1.0 - beta_one ** step_count) / (jnp.sqrt(second_moment / (1.0 - beta_two ** step_count)) + adam_eps)
    new_master = master - learn_rate * (update + decay_rate * master)
    return (predictions, new_master, first_moment, second_moment)
```

```python
import math

import jax
import jax.numpy as jnp
from jax import lax
from jax.sharding import PartitionSpec as P

D = 8192
SPEC = 8


norm_eps = 1e-06
beta_one = 0.9
beta_two = 0.95
adam_eps = 1e-08
learn_rate = 0.01
decay_rate = 0.1
step_count = 10


def adam_update(master, moment_one, moment_two, gradient):
    first_moment = beta_one * moment_one + (1.0 - beta_one) * gradient
    second_moment = beta_two * moment_two + (1.0 - beta_two) * gradient * gradient
    update = (
        first_moment
        / (1.0 - beta_one**step_count)
        / (jnp.sqrt(second_moment / (1.0 - beta_two**step_count)) + adam_eps)
    )
    return (master - learn_rate * (update + decay_rate * master), first_moment, second_moment)


def local(
    attn_out,
    o_proj,
    residual,
    norm_gain,
    dest_group,
    accept_count,
    target_values,
    master,
    moment_one,
    moment_two,
):
    group_count = lax.axis_size("grp")
    shard_count = lax.axis_size("tp")
    row_count = attn_out.shape[0]
    capacity = 2 * row_count // group_count
    tokens_all = row_count * group_count
    g, t = lax.axis_index("grp"), lax.axis_index("tp")
    weight = lax.all_gather(master.astype(jnp.bfloat16), "grp", axis=0, tiled=True)
    hidden = residual.astype(jnp.float32) + jnp.dot(
        lax.all_gather(attn_out, "tp", axis=1, tiled=True),
        o_proj,
        preferred_element_type=jnp.float32,
    )
    squares = lax.psum(jnp.sum(hidden * hidden, axis=1), "tp")
    scale_row = lax.rsqrt(squares / D + norm_eps)
    feature = (hidden * scale_row[:, None] * norm_gain[None, :]).astype(jnp.bfloat16)
    partial = lax.dot_general(
        feature, weight, (((1,), (1,)), ((), ())), preferred_element_type=jnp.float32
    )
    values = lax.psum(partial, "tp")

    target_group = dest_group[:, 0]
    onehot = target_group[:, None] == jnp.arange(group_count, dtype=jnp.int32)[None, :]
    before = jnp.tril(jnp.ones((row_count, row_count), jnp.bfloat16), -1)
    earlier = jnp.dot(before, onehot.astype(jnp.bfloat16), preferred_element_type=jnp.float32)
    ranking = jnp.sum(jnp.where(onehot, earlier, 0.0), axis=1).astype(jnp.int32)
    accepted = (
        jnp.arange(row_count, dtype=jnp.int32) % SPEC < jnp.repeat(accept_count, SPEC)
    ).astype(jnp.float32)
    errors = (accepted[:, None] * (values - target_values.astype(jnp.float32))).astype(
        jnp.bfloat16
    )
    partial_grad = lax.dot_general(
        errors, feature, (((0,), (0,)), ((), ())), preferred_element_type=jnp.float32
    )
    gradient = lax.psum_scatter(partial_grad, "grp", scatter_dimension=0, tiled=True)
    gradient = gradient / math.sqrt(tokens_all)

    rows_out = values.astype(jnp.bfloat16)
    blocks = []
    for turn in range(2):
        dest = 2 * t + (turn + g) % 2
        spot = jnp.where(target_group == dest, ranking, -1)
        pick = (jnp.arange(capacity, dtype=jnp.int32)[:, None] == spot[None, :]).astype(jnp.bfloat16)
        block = jnp.dot(pick, rows_out, preferred_element_type=jnp.float32).astype(jnp.bfloat16)
        pairs = [
            (a * shard_count + b, (2 * b + (turn + a) % 2) * shard_count + a // 2)
            for a in range(group_count)
            for b in range(shard_count)
        ]
        blocks.append(lax.ppermute(block, ("grp", "tp"), pairs))
    first = jnp.where(g % 2 == 0, blocks[0], blocks[1])
    second = jnp.where(g % 2 == 0, blocks[1], blocks[0])
    predictions = jnp.concatenate([first, second], axis=0)
    new_master, first_moment, second_moment = adam_update(master, moment_one, moment_two, gradient)
    return (predictions, new_master, first_moment, second_moment)


def solution(mesh):
    in_specs = (
        P("grp", "tp"),
        P(None, "tp"),
        P("grp", "tp"),
        P("tp"),
        P("grp", None),
        P("grp"),
        P("grp", None),
        P("grp", "tp"),
        P("grp", "tp"),
        P("grp", "tp"),
    )
    out_specs = (P(("grp", "tp"), None), P("grp", "tp"), P("grp", "tp"), P("grp", "tp"))
    return jax.shard_map(local, mesh=mesh, in_specs=in_specs, out_specs=out_specs, check_vma=False)
```

```python
import functools
import math

import jax
import jax.numpy as jnp
from jax import lax
from jax.experimental import pallas as pl
from jax.experimental.pallas import tpu as pltpu
from jax.sharding import PartitionSpec as P

D = 8192
SPEC = 8


norm_eps = 1e-06
beta_one = 0.9
beta_two = 0.95
adam_eps = 1e-08
learn_rate = 0.01
decay_rate = 0.1
step_count = 10

MESH = pl.DeviceIdType.MESH
F32 = jnp.float32
BF16 = jnp.bfloat16

NZ = 4
CORES = 2
CHUNK = 256
EXTRA = 128


def adam_update(master, moment_one, moment_two, gradient):
    first_moment = beta_one * moment_one + (1.0 - beta_one) * gradient
    second_moment = beta_two * moment_two + (1.0 - beta_two) * gradient * gradient
    update = (
        first_moment
        / (1.0 - beta_one**step_count)
        / (jnp.sqrt(second_moment / (1.0 - beta_two**step_count)) + adam_eps)
    )
    return (master - learn_rate * (update + decay_rate * master), first_moment, second_moment)


def with_column(values, column):
    high = column.astype(BF16).astype(F32)
    low = column - high
    lane = lax.broadcasted_iota(jnp.int32, (values.shape[0], EXTRA), 1)
    extra = jnp.where(lane < EXTRA // 2, high, low)
    return values.astype(BF16), extra.astype(BF16)


def column_of(extra):
    extra = extra.astype(F32)
    return extra[:, 0:1] + extra[:, EXTRA // 2 : EXTRA // 2 + 1]


def kernel(
    attn,
    o_proj,
    residual,
    gain,
    dest,
    accept,
    target,
    master,
    pred,
    grad,
    a_all,
    w_own,
    res_own,
    tgt_own,
    mst_own,
    mst_all,
    u_all,
    part,
    pair_in,
    pair_sum,
    z_in,
    val_all,
    g_sum,
    g_out,
    g_in,
    p_out,
    spot,
    load_sem,
    ag_send,
    ag_recv,
    vs_send,
    vs_recv,
    m_send,
    m_recv,
    g_send,
    g_recv,
    p_send,
    p_recv,
):
    rows, width = attn.shape
    cols = o_proj.shape[1]
    kvw = target.shape[1]
    groups = lax.axis_size("grp")
    own_rows = kvw // groups
    capacity = 2 * rows // groups
    chunks = rows // CHUNK
    half = CHUNK // CORES
    sub = half // NZ
    g, t = lax.axis_index("grp"), lax.axis_index("tp")
    z, core = t // CORES, t % CORES
    other = 1 - core
    z_up, z_down, z_far = (z + 1) % NZ, (z + NZ - 1) % NZ, (z + 2) % NZ
    pred_shard = g // 2
    up, down, far = (g, z_up * CORES + core), (g, z_down * CORES + core), (g, z_far * CORES + core)
    sibling = (g, z * CORES + other)

    def is_self(j):
        return jnp.logical_and(t == pred_shard, g % 2 == j)

    sends = []

    def copy_to(src, dst, send_sem, recv_sem, device):
        copy = pltpu.make_async_remote_copy(
            src_ref=src,
            dst_ref=dst,
            send_sem=send_sem,
            recv_sem=recv_sem,
            device_id=device,
            device_id_type=MESH,
        )
        copy.start()
        sends.append(copy)

    def wait_for(dst, send_sem, recv_sem, device):
        pltpu.make_async_remote_copy(
            src_ref=dst,
            dst_ref=dst,
            send_sem=send_sem,
            recv_sem=recv_sem,
            device_id=device,
            device_id_type=MESH,
        ).wait_recv()

    def block(zz, cc, start, size):
        return a_all.at[
            pl.ds(start, size), pl.ds(pl.multiple_of((zz * CORES + cc) * width, width), width)
        ]

    loads = [
        pltpu.make_async_copy(master, mst_own, load_sem.at[0]),
        pltpu.make_async_copy(attn, block(z, core, 0, rows), load_sem.at[1]),
        pltpu.make_async_copy(residual, res_own, load_sem.at[2]),
        pltpu.make_async_copy(target, tgt_own, load_sem.at[3]),
    ]
    pieces = 4
    depth = o_proj.shape[0] // pieces
    for k in range(pieces):
        loads.append(
            pltpu.make_async_copy(
                o_proj.at[pl.ds(k * depth, depth)],
                w_own.at[pl.ds(k * depth, depth)],
                load_sem.at[4 + k],
            )
        )
    for load in loads:
        load.start()

    barrier = pltpu.get_barrier_semaphore()

    def greet(device):
        pl.semaphore_signal(barrier, inc=1, device_id=device, device_id_type=MESH)

    for device in (up, down, far, sibling):
        greet(device)
    for k in range(1, groups):
        greet(((g + k) % groups, t))
    for j in range(2):

        @pl.when(jnp.logical_not(is_self(j)))
        def _():
            greet((2 * t + j, pred_shard))

    pl.semaphore_wait(barrier, 4 + groups - 1 + 2 - (t == pred_shard).astype(jnp.int32))

    def send_own(i):
        start = i * CHUNK
        src = attn.at[pl.ds(start, CHUNK)]
        dst = block(z, core, start, CHUNK)
        copy_to(src, dst, ag_send.at[i, 0], ag_recv.at[i, 0], up)
        copy_to(src, dst, ag_send.at[i, 1], ag_recv.at[i, 1], down)
        copy_to(src, dst, ag_send.at[i, 2], ag_recv.at[i, 2], sibling)

    send_own(0)
    send_own(1)

    def mst_rows(gg):
        return mst_all.at[pl.ds(pl.multiple_of(gg * own_rows, own_rows), own_rows)]

    loads[0].wait()
    mst_rows(g)[...] = mst_own[...].astype(BF16)
    for k in range(1, groups):
        copy_to(mst_rows(g), mst_rows(g), m_send.at[k], m_recv.at[k], ((g + k) % groups, t))

    tile = 256
    for n in range(rows // tile):
        here = pl.ds(n * tile, tile)
        kinds = lax.broadcasted_iota(jnp.int32, (groups, rows), 0)
        onehot = (kinds == dest[...]).astype(F32).astype(BF16)
        earlier_rows = lax.broadcasted_iota(jnp.int32, (rows, tile), 0)
        these_rows = lax.broadcasted_iota(jnp.int32, (rows, tile), 1) + n * tile
        before = (earlier_rows < these_rows).astype(F32).astype(BF16)
        earlier = jnp.dot(onehot, before, preferred_element_type=F32)
        dest_here = dest[:, here]
        mine = lax.broadcasted_iota(jnp.int32, (groups, tile), 0) == dest_here
        rank = jnp.sum(jnp.where(mine, earlier, 0.0), axis=0, keepdims=True)
        spot[:, here] = dest_here * capacity + rank.astype(jnp.int32)

    def pass_on(i):
        start = i * CHUNK
        wait_for(block(z_down, core, start, CHUNK), ag_send.at[i, 0], ag_recv.at[i, 0], down)
        src = block(z_down, core, start, CHUNK // 2)
        copy_to(src, src, ag_send.at[i, 3], ag_recv.at[i, 3], up)
        src = block(z_down, core, start, CHUNK)
        copy_to(src, src, ag_send.at[i, 4], ag_recv.at[i, 4], sibling)
        wait_for(block(z_up, core, start, CHUNK), ag_send.at[i, 1], ag_recv.at[i, 1], up)
        src = block(z_up, core, start + CHUNK // 2, CHUNK // 2)
        copy_to(src, src, ag_send.at[i, 5], ag_recv.at[i, 5], down)
        src = block(z_up, core, start, CHUNK)
        copy_to(src, src, ag_send.at[i, 6], ag_recv.at[i, 6], sibling)

    def pass_far(i):
        start = i * CHUNK
        wait_for(block(z_far, core, start, CHUNK // 2), ag_send.at[i, 3], ag_recv.at[i, 3], down)
        wait_for(
            block(z_far, core, start + CHUNK // 2, CHUNK // 2), ag_send.at[i, 5], ag_recv.at[i, 5], up
        )
        src = block(z_far, core, start, CHUNK)
        copy_to(src, src, ag_send.at[i, 7], ag_recv.at[i, 7], sibling)

    def multiply(i):
        start = i * CHUNK
        wait_for(block(z, other, start, CHUNK), ag_send.at[i, 2], ag_recv.at[i, 2], sibling)
        wait_for(block(z_down, other, start, CHUNK), ag_send.at[i, 4], ag_recv.at[i, 4], sibling)
        wait_for(block(z_up, other, start, CHUNK), ag_send.at[i, 6], ag_recv.at[i, 6], sibling)
        wait_for(block(z_far, other, start, CHUNK), ag_send.at[i, 7], ag_recv.at[i, 7], sibling)
        if i == 0:
            for load in loads[1:]:
                load.wait()
            for k in range(1, groups):
                gg = (g + groups - k) % groups
                wait_for(mst_rows(gg), m_send.at[k], m_recv.at[k], (gg, t))
        here = pl.ds(start, CHUNK)

        def columns(n, squares):
            there = pl.ds(pl.multiple_of(n * 256, 256), 256)
            hidden = jnp.dot(a_all[here, :], w_own[:, there], preferred_element_type=F32)
            hidden = hidden + res_own[here, there].astype(F32)
            u_all[here, there] = (hidden * gain[:, there]).astype(BF16)
            squared = hidden * hidden
            return squares + squared[:, :128] + squared[:, 128:]

        squares = lax.fori_loop(0, cols // 256, columns, jnp.zeros((CHUNK, 128), F32))
        values = lax.dot_general(
            u_all[here, :],
            mst_all[...],
            (((1,), (1,)), ((), ())),
            preferred_element_type=F32,
        )
        main, extra = with_column(values, jnp.sum(squares, axis=1, keepdims=True))
        part[here, :kvw] = main
        part[here, kvw:] = extra
        src = part.at[pl.ds(pl.multiple_of(start + other * half, half), half)]
        copy_to(src, pair_in.at[i], vs_send.at[i, 0], vs_recv.at[i, 0], sibling)

    def add_pair(i):
        start = i * CHUNK
        wait_for(pair_in.at[i], vs_send.at[i, 0], vs_recv.at[i, 0], sibling)
        mine = pl.ds(pl.multiple_of(start + core * half, half), half)
        values = part[mine, :kvw].astype(F32) + pair_in[i, :, :kvw].astype(F32)
        column = column_of(part[mine, kvw:]) + column_of(pair_in[i, :, kvw:])
        main, extra = with_column(values, column)
        pair_sum[i, :, :kvw] = main
        pair_sum[i, :, kvw:] = extra
        for k in range(1, NZ):
            zz = (z + k) % NZ
            src = pair_sum.at[i, pl.ds(pl.multiple_of(zz * sub, sub), sub)]
            copy_to(
                src, z_in.at[i, k], vs_send.at[i, k], vs_recv.at[i, k], (g, zz * CORES + core)
            )

    def own_part(i, zz, cc):
        return pl.ds(pl.multiple_of(i * CHUNK + cc * half + zz * sub, sub), sub)

    def finish_values(i):
        mine = pl.ds(pl.multiple_of(z * sub, sub), sub)
        values = pair_sum[i, mine, :kvw].astype(F32)
        column = column_of(pair_sum[i, mine, kvw:])
        for k in range(1, NZ):
            zz = (z + NZ - k) % NZ
            wait_for(z_in.at[i, k], vs_send.at[i, k], vs_recv.at[i, k], (g, zz * CORES + core))
            values = values + z_in[i, k, :, :kvw].astype(F32)
            column = column + column_of(z_in[i, k, :, kvw:])
        scale = lax.rsqrt(column / D + norm_eps)
        main, extra = with_column(values * scale, scale)
        here = own_part(i, z, core)
        val_all[here, :kvw] = main
        val_all[here, kvw:] = extra
        for k in range(1, NZ):
            zz = (z + k) % NZ
            src = val_all.at[here]
            copy_to(
                src, src, vs_send.at[i, 3 + k], vs_recv.at[i, 3 + k], (g, zz * CORES + core)
            )

    def pass_values(i):
        for k in range(1, NZ):
            zz = (z + NZ - k) % NZ
            dst = val_all.at[own_part(i, zz, core)]
            wait_for(dst, vs_send.at[i, 3 + k], vs_recv.at[i, 3 + k], (g, zz * CORES + core))
        src = val_all.at[pl.ds(pl.multiple_of(i * CHUNK + core * half, half), half)]
        copy_to(src, src, vs_send.at[i, 7], vs_recv.at[i, 7], sibling)

    def add_gradient(i):
        start = i * CHUNK
        dst = val_all.at[pl.ds(pl.multiple_of(start + other * half, half), half)]
        wait_for(dst, vs_send.at[i, 7], vs_recv.at[i, 7], sibling)
        here = pl.ds(start, CHUNK)
        requests = accept.shape[1]
        row = lax.broadcasted_iota(jnp.int32, (CHUNK, requests), 0) + start
        request = lax.broadcasted_iota(jnp.int32, (CHUNK, requests), 1)
        taken = jnp.sum(
            jnp.where(row // SPEC == request, accept[...], 0).astype(F32), axis=1, keepdims=True
        )
        place = (lax.broadcasted_iota(jnp.int32, (CHUNK, 1), 0) % SPEC).astype(F32)
        weight = jnp.where(place < taken, column_of(val_all[here, kvw:]), 0.0)
        errors = weight * (val_all[here, :kvw].astype(F32) - tgt_own[here, :].astype(F32))
        product = lax.dot_general(
            errors.T.astype(BF16),
            u_all[here, :],
            (((1,), (0,)), ((), ())),
            preferred_element_type=F32,
        )
        if i == 0:
            g_sum[...] = product
        elif i < chunks - 1:
            g_sum[...] += product
        else:
            total = g_sum[...] + product
            g_sum[...] = total
            g_out[...] = total.astype(BF16)

    for it in range(chunks + 5):
        for stage, lag in (
            (pass_on, 0),
            (pass_far, 1),
            (add_pair, 2),
            (finish_values, 3),
            (pass_values, 4),
            (add_gradient, 5),
            (multiply, 1),
        ):
            i = it - lag
            if 0 <= i < chunks:
                stage(i)
            if stage is pass_on and 0 <= i + 2 < chunks and i >= 0:
                send_own(i + 2)

    def g_rows(gg):
        return pl.ds(pl.multiple_of(gg * own_rows, own_rows), own_rows)

    for k in range(1, groups):
        gg = (g + k) % groups
        copy_to(g_out.at[g_rows(gg)], g_in.at[k], g_send.at[k], g_recv.at[k], (gg, t))

    slot = lax.broadcasted_iota(jnp.int32, (2 * capacity, rows), 0) + 2 * t * capacity
    pick = (slot == spot[...]).astype(F32).astype(BF16)
    p_out[...] = jnp.dot(pick, val_all[:, :kvw], preferred_element_type=F32).astype(BF16)

    def pred_copy(j):
        return pltpu.make_async_remote_copy(
            src_ref=p_out.at[pl.ds(j * capacity, capacity)],
            dst_ref=pred.at[pl.ds(pl.multiple_of((g % 2) * capacity, capacity), capacity)],
            send_sem=p_send.at[j],
            recv_sem=p_recv.at[g % 2],
            device_id=(2 * t + j, pred_shard),
            device_id_type=MESH,
        )

    def pred_local(j):
        return pltpu.make_async_copy(
            p_out.at[pl.ds(j * capacity, capacity)],
            pred.at[pl.ds(j * capacity, capacity)],
            p_send.at[j],
        )

    for j in range(2):

        @pl.when(is_self(j))
        def _():
            pred_local(j).start()

        @pl.when(jnp.logical_not(is_self(j)))
        def _():
            pred_copy(j).start()

    total = g_sum[g_rows(g), :]
    for k in range(1, groups):
        gg = (g + groups - k) % groups
        wait_for(g_in.at[k], g_send.at[k], g_recv.at[k], (gg, t))
        total = total + g_in[k].astype(F32)
    grad[...] = total * (1.0 / math.sqrt(rows * groups))

    for j in range(2):

        @pl.when(is_self(j))
        def _():
            pred_local(j).wait()

        @pl.when(jnp.logical_not(is_self(j)))
        def _():
            pred_copy(j).wait_send()
            wait_for(
                pred.at[pl.ds(j * capacity, capacity)],
                p_send.at[j],
                p_recv.at[j],
                (2 * t + j, pred_shard),
            )

    for copy in sends:
        copy.wait_send()


def local(
    attn_out,
    o_proj,
    residual,
    norm_gain,
    dest_group,
    accept_count,
    target_values,
    master,
    moment_one,
    moment_two,
):
    groups = lax.axis_size("grp")
    rows, width = attn_out.shape
    depth, cols = o_proj.shape
    kvw = target_values.shape[1]
    own_rows = master.shape[0]
    chunks = rows // CHUNK
    half = CHUNK // CORES
    sub = half // NZ
    wide = kvw + EXTRA
    slots = 2 * (2 * rows // groups)
    any_spec = pl.BlockSpec(memory_space=pl.ANY)
    vmem_spec = pl.BlockSpec(memory_space=pltpu.VMEM)
    dma = pltpu.SemaphoreType.DMA
    pred, grad = pl.pallas_call(
        kernel,
        out_shape=(
            jax.ShapeDtypeStruct((slots, kvw), BF16),
            jax.ShapeDtypeStruct((own_rows, cols), F32),
        ),
        in_specs=[any_spec, any_spec, any_spec, vmem_spec, vmem_spec, vmem_spec, any_spec, any_spec],
        out_specs=(any_spec, vmem_spec),
        scratch_shapes=[
            pltpu.VMEM((rows, depth), BF16),
            pltpu.VMEM((depth, cols), BF16),
            pltpu.VMEM((rows, cols), BF16),
            pltpu.VMEM((rows, kvw), BF16),
            pltpu.VMEM((own_rows, cols), F32),
            pltpu.VMEM((kvw, cols), BF16),
            pltpu.VMEM((rows, cols), BF16),
            pltpu.VMEM((rows, wide), BF16),
            pltpu.VMEM((chunks, half, wide), BF16),
            pltpu.VMEM((chunks, half, wide), BF16),
            pltpu.VMEM((chunks, NZ, sub, wide), BF16),
            pltpu.VMEM((rows, wide), BF16),
            pltpu.VMEM((kvw, cols), F32),
            pltpu.VMEM((kvw, cols), BF16),
            pltpu.VMEM((groups, own_rows, cols), BF16),
            pltpu.VMEM((slots, kvw), BF16),
            pltpu.VMEM((1, rows), jnp.int32),
            dma((8,)),
            dma((chunks, 8)),
            dma((chunks, 8)),
            dma((chunks, 8)),
            dma((chunks, 8)),
            dma((groups,)),
            dma((groups,)),
            dma((groups,)),
            dma((groups,)),
            dma((2,)),
            dma((2,)),
        ],
        compiler_params=pltpu.CompilerParams(
            collective_id=0, has_side_effects=True, vmem_limit_bytes=56 * 2**20
        ),
        cost_estimate=pl.CostEstimate(
            flops=2 * rows * cols * (depth + 2 * kvw),
            bytes_accessed=2 * (depth * cols + rows * (cols + width + kvw)),
            transcendentals=0,
        ),
        name="step",
    )(
        attn_out,
        o_proj,
        residual,
        norm_gain.reshape(1, cols),
        dest_group.reshape(1, rows),
        accept_count.reshape(1, rows // SPEC),
        target_values,
        master,
    )
    new_master, first_moment, second_moment = adam_update(master, moment_one, moment_two, grad)
    return (pred, new_master, first_moment, second_moment)


def solution(mesh):
    in_specs = (
        P("grp", "tp"),
        P(None, "tp"),
        P("grp", "tp"),
        P("tp"),
        P("grp", None),
        P("grp"),
        P("grp", None),
        P("grp", "tp"),
        P("grp", "tp"),
        P("grp", "tp"),
    )
    out_specs = (P(("grp", "tp"), None), P("grp", "tp"), P("grp", "tp"), P("grp", "tp"))
    return jax.shard_map(local, mesh=mesh, in_specs=in_specs, out_specs=out_specs, check_vma=False)
```

```python
import functools
import math

import jax
import jax.numpy as jnp
from jax import lax
from jax.experimental import pallas as pl
from jax.experimental.pallas import tpu as pltpu
from jax.sharding import PartitionSpec as P

D = 8192
SPEC = 8


norm_eps = 1e-06
beta_one = 0.9
beta_two = 0.95
adam_eps = 1e-08
learn_rate = 0.01
decay_rate = 0.1
step_count = 10

MESH = pl.DeviceIdType.MESH
F32 = jnp.float32
BF16 = jnp.bfloat16

NX, NY, NZ, CORES = 4, 4, 4, 2
SIZES = (384, 256, 256, 128)
STARTS = tuple(sum(SIZES[:i]) for i in range(len(SIZES)))
CHUNKS = len(SIZES)
LANES = 128
TILE = 256
OWN, UP, DOWN, FAR = range(4)


def adam_update(master, moment_one, moment_two, gradient):
    first_moment = beta_one * moment_one + (1.0 - beta_one) * gradient
    second_moment = beta_two * moment_two + (1.0 - beta_two) * gradient * gradient
    update = (
        first_moment
        / (1.0 - beta_one**step_count)
        / (jnp.sqrt(second_moment / (1.0 - beta_two**step_count)) + adam_eps)
    )
    return (master - learn_rate * (update + decay_rate * master), first_moment, second_moment)


def finish_kernel(pred, grad, master, one, two, pred_out, master_out, one_out, two_out):
    pred_out[...] = pred[...]
    master_out[...], one_out[...], two_out[...] = adam_update(
        master[...], one[...], two[...], grad[...]
    )


def kernel(
    attn,
    o_proj,
    residual,
    gain,
    dest,
    accept,
    target,
    master,
    pred,
    grad,
    a_all,
    w_own,
    res_own,
    tgt_own,
    mst_own,
    mst_all,
    u_all,
    near,
    part,
    pair_in,
    pair_sum,
    z_in,
    val_all,
    sq_out,
    sq_pair,
    sq_sum,
    sq_z,
    scales,
    g_sum,
    g_one_out,
    g_two_out,
    g_one_in,
    g_two_in,
    h_one,
    h_two,
    h_one_out,
    h_two_out,
    h_one_in,
    h_two_in,
    p_out,
    spot,
    load_sem,
    ag_send,
    ag_recv,
    vs_send,
    vs_recv,
    sq_send,
    sq_recv,
    m_send,
    m_recv,
    g_send,
    g_recv,
    p_send,
    p_recv,
):
    rows, width = attn.shape
    cols = o_proj.shape[1]
    kvw = target.shape[1]
    groups = NX * NY
    own_rows = kvw // groups
    side = cols // 2
    capacity = 2 * rows // groups
    g, t = lax.axis_index("grp"), lax.axis_index("tp")
    z, core = t // CORES, t % CORES
    y, x = g // NX, g % NX
    other = 1 - core

    def along_z(k):
        return (g, ((z + k) % NZ) * CORES + core)

    def along_x(k):
        return (y * NX + (x + k) % NX, t)

    def along_y(k):
        return (((y + k) % NY) * NX + x, t)

    up, down, far = along_z(1), along_z(NZ - 1), along_z(2)
    sibling = (g, z * CORES + other)

    def pred_to(j):
        turn = z + x if j == 0 else 2 * NY - z - x
        return ((y + turn) % NY) * NX + 2 * core + j, g // 2

    def pred_from(j):
        source = 2 * t + j
        source_y, source_x = source // NX, source % NX
        odd = x % 2
        turn = (y - source_y + NY) * (1 - odd) + (source_y - y + NY) * odd
        return source, ((turn - source_x + 2 * NZ) % NZ) * CORES + x // 2

    def is_self(device):
        return jnp.logical_and(device[0] == g, device[1] == t)

    sends = []

    def copy_to(src, dst, send_sem, recv_sem, device):
        copy = pltpu.make_async_remote_copy(
            src_ref=src,
            dst_ref=dst,
            send_sem=send_sem,
            recv_sem=recv_sem,
            device_id=device,
            device_id_type=MESH,
        )
        copy.start()
        sends.append(copy)

    def wait_for(dst, send_sem, recv_sem, device):
        pltpu.make_async_remote_copy(
            src_ref=dst,
            dst_ref=dst,
            send_sem=send_sem,
            recv_sem=recv_sem,
            device_id=device,
            device_id_type=MESH,
        ).wait_recv()

    def place(which, cc):
        return pl.ds(pl.multiple_of((which * CORES + cc) * width, width), width)

    def block(which, cc, start, size):
        return a_all.at[pl.ds(start, size), place(which, cc)]

    loads = [
        pltpu.make_async_copy(master, mst_own, load_sem.at[0]),
        pltpu.make_async_copy(attn, block(OWN, core, 0, rows), load_sem.at[1]),
        pltpu.make_async_copy(residual, res_own, load_sem.at[2]),
        pltpu.make_async_copy(target, tgt_own, load_sem.at[3]),
    ]
    for which, step in ((OWN, 0), (UP, 1), (DOWN, NZ - 1), (FAR, 2)):
        for cc in range(CORES):
            first = ((z + step) % NZ * CORES + cc) * width
            loads.append(
                pltpu.make_async_copy(
                    o_proj.at[pl.ds(pl.multiple_of(first, width), width)],
                    w_own.at[place(which, cc)],
                    load_sem.at[4 + which * CORES + cc],
                )
            )
    for load in loads:
        load.start()

    barrier = pltpu.get_barrier_semaphore()

    def greet(device):
        pl.semaphore_signal(barrier, inc=1, device_id=device, device_id_type=MESH)

    for k in range(1, NZ):
        greet(along_z(k))
        greet(along_x(k))
        greet(along_y(k))
    greet(sibling)
    expected = jnp.int32(3 * (NZ - 1) + 1)
    for j in range(2):

        @pl.when(jnp.logical_not(is_self(pred_from(j))))
        def _():
            greet(pred_from(j))

        expected = expected + 1 - is_self(pred_to(j)).astype(jnp.int32)
    pl.semaphore_wait(barrier, expected)

    def send_own(i):
        start, size = STARTS[i], SIZES[i]
        src = attn.at[pl.ds(start, size)]
        copy_to(src, block(DOWN, core, start, size), ag_send.at[i, 0], ag_recv.at[i, 0], up)
        copy_to(src, block(UP, core, start, size), ag_send.at[i, 1], ag_recv.at[i, 1], down)
        copy_to(src, block(OWN, core, start, size), ag_send.at[i, 2], ag_recv.at[i, 2], sibling)

    send_own(0)
    send_own(1)

    def mst_rows(first, count):
        return mst_all.at[pl.ds(pl.multiple_of(first * own_rows, own_rows), count * own_rows)]

    loads[0].wait()
    mst_rows(g, 1)[...] = mst_own[...].astype(BF16)
    for k in range(1, NX):
        copy_to(mst_rows(g, 1), mst_rows(g, 1), m_send.at[0, k], m_recv.at[0, k], along_x(k))

    for n in range(rows // TILE):
        here = pl.ds(n * TILE, TILE)
        kinds = lax.broadcasted_iota(jnp.int32, (groups, rows), 0)
        onehot = (kinds == dest[...]).astype(F32).astype(BF16)
        earlier_rows = lax.broadcasted_iota(jnp.int32, (rows, TILE), 0)
        these_rows = lax.broadcasted_iota(jnp.int32, (rows, TILE), 1) + n * TILE
        before = (earlier_rows < these_rows).astype(F32).astype(BF16)
        earlier = jnp.dot(onehot, before, preferred_element_type=F32)
        dest_here = dest[:, here]
        mine = lax.broadcasted_iota(jnp.int32, (groups, TILE), 0) == dest_here
        rank = jnp.sum(jnp.where(mine, earlier, 0.0), axis=0, keepdims=True)
        spot[:, here] = dest_here * capacity + rank.astype(jnp.int32)

    for k in range(1, NX):
        source = along_x(NX - k)
        wait_for(mst_rows(source[0], 1), m_send.at[0, k], m_recv.at[0, k], source)
    for k in range(1, NY):
        src = mst_rows(y * NX, NX)
        copy_to(src, src, m_send.at[1, k], m_recv.at[1, k], along_y(k))

    def pass_on(i):
        start, size = STARTS[i], SIZES[i]
        part_size = size // 2
        src = block(DOWN, core, start, size)
        wait_for(src, ag_send.at[i, 0], ag_recv.at[i, 0], down)
        copy_to(
            block(DOWN, core, start, part_size),
            block(FAR, core, start, part_size),
            ag_send.at[i, 3],
            ag_recv.at[i, 3],
            up,
        )
        copy_to(src, src, ag_send.at[i, 4], ag_recv.at[i, 4], sibling)
        src = block(UP, core, start, size)
        wait_for(src, ag_send.at[i, 1], ag_recv.at[i, 1], up)
        copy_to(
            block(UP, core, start + part_size, part_size),
            block(FAR, core, start + part_size, part_size),
            ag_send.at[i, 5],
            ag_recv.at[i, 5],
            down,
        )
        copy_to(src, src, ag_send.at[i, 6], ag_recv.at[i, 6], sibling)
        if i + 2 < CHUNKS:
            send_own(i + 2)

    def pass_far(i):
        start, size = STARTS[i], SIZES[i]
        part_size = size // 2
        wait_for(
            block(FAR, core, start, part_size), ag_send.at[i, 3], ag_recv.at[i, 3], down
        )
        wait_for(
            block(FAR, core, start + part_size, part_size), ag_send.at[i, 5], ag_recv.at[i, 5], up
        )
        src = block(FAR, core, start, size)
        copy_to(src, src, ag_send.at[i, 7], ag_recv.at[i, 7], sibling)

    def multiply(i):
        start, size = STARTS[i], SIZES[i]
        here = pl.ds(start, size)
        last = i == CHUNKS - 1
        depth = FAR * CORES * width
        for which, sem in ((OWN, 2), (DOWN, 4), (UP, 6)):
            wait_for(block(which, other, start, size), ag_send.at[i, sem], ag_recv.at[i, sem], sibling)
        if i == 0:
            for load in loads[1:]:
                load.wait()

        def near_columns(n, carry):
            there = pl.ds(pl.multiple_of(n * TILE, TILE), TILE)
            near[:, there] = jnp.dot(
                a_all[here, :depth], w_own[:depth, there], preferred_element_type=F32
            )
            return carry

        if last:
            lax.fori_loop(0, cols // TILE, near_columns, 0)
        wait_for(block(FAR, other, start, size), ag_send.at[i, 7], ag_recv.at[i, 7], sibling)

        def columns(n, squares):
            there = pl.ds(pl.multiple_of(n * TILE, TILE), TILE)
            if last:
                hidden = near[:, there] + jnp.dot(
                    a_all[here, depth:], w_own[depth:, there], preferred_element_type=F32
                )
            else:
                hidden = jnp.dot(a_all[here, :], w_own[:, there], preferred_element_type=F32)
            hidden = hidden + res_own[here, there].astype(F32)
            u_all[here, there] = (hidden * gain[:, there]).astype(BF16)
            squared = hidden * hidden
            return squares + squared[:, :LANES] + squared[:, LANES:]

        squares = lax.fori_loop(0, cols // TILE, columns, jnp.zeros((size, LANES), F32))
        total = jnp.sum(squares.T, axis=0, keepdims=True)
        sq_out[i, :, :size] = jnp.broadcast_to(total, (8, size))
        copy_to(sq_out.at[i], sq_pair.at[i], sq_send.at[i, 0], sq_recv.at[i, 0], sibling)
        if i == 0:
            for k in range(1, NY):
                source = (y + NY - k) % NY
                wait_for(
                    mst_rows(source * NX, NX), m_send.at[1, k], m_recv.at[1, k], along_y(NY - k)
                )
        part[here, :] = lax.dot_general(
            u_all[here, :],
            mst_all[...],
            (((1,), (1,)), ((), ())),
            preferred_element_type=F32,
        ).astype(BF16)
        half = size // CORES
        src = part.at[pl.ds(pl.multiple_of(start + other * half, half), half)]
        dst = pair_in.at[pl.ds(start // CORES, half)]
        copy_to(src, dst, vs_send.at[i, 0], vs_recv.at[i, 0], sibling)

    def add_pair(i):
        start, size = STARTS[i], SIZES[i]
        half = size // CORES
        sub = half // NZ
        first = start // CORES
        wait_for(sq_pair.at[i], sq_send.at[i, 0], sq_recv.at[i, 0], sibling)
        sq_sum[i] = sq_out[i] + sq_pair[i]
        for k in range(1, NZ):
            copy_to(sq_sum.at[i], sq_z.at[i, k], sq_send.at[i, k], sq_recv.at[i, k], along_z(k))
        here = pl.ds(first, half)
        wait_for(pair_in.at[here], vs_send.at[i, 0], vs_recv.at[i, 0], sibling)
        mine = pl.ds(pl.multiple_of(start + core * half, half), half)
        pair_sum[here, :] = (part[mine, :].astype(F32) + pair_in[here, :].astype(F32)).astype(BF16)
        for k in range(1, NZ):
            src = pair_sum.at[pl.ds(pl.multiple_of(first + (z + k) % NZ * sub, sub), sub)]
            dst = z_in.at[k, pl.ds(start // (CORES * NZ), sub)]
            copy_to(src, dst, vs_send.at[i, k], vs_recv.at[i, k], along_z(k))

    def own_part(i, zz):
        sub = SIZES[i] // (CORES * NZ)
        return pl.ds(pl.multiple_of(STARTS[i] + (core * NZ + zz) * sub, sub), sub)

    def finish_values(i):
        start, size = STARTS[i], SIZES[i]
        sub = size // (CORES * NZ)
        total = sq_sum[i]
        for k in range(1, NZ):
            wait_for(sq_z.at[i, k], sq_send.at[i, k], sq_recv.at[i, k], along_z(NZ - k))
            total = total + sq_z[i, k]
        scale = lax.rsqrt(total[:1, :size] / D + norm_eps)
        scales[pl.ds(start, size), :] = jnp.broadcast_to(scale, (LANES, size)).T
        mine = pl.ds(pl.multiple_of(start // CORES + z * sub, sub), sub)
        there = pl.ds(start // (CORES * NZ), sub)
        values = pair_sum[mine, :].astype(F32)
        for k in range(1, NZ):
            wait_for(z_in.at[k, there], vs_send.at[i, k], vs_recv.at[i, k], along_z(NZ - k))
            values = values + z_in[k, there, :].astype(F32)
        here = own_part(i, z)
        val_all[here, :] = (values * scales[here, :1]).astype(BF16)
        src = val_all.at[here]
        for k in range(1, NZ):
            copy_to(src, src, vs_send.at[i, 3 + k], vs_recv.at[i, 3 + k], along_z(k))

    def pass_values(i):
        half = SIZES[i] // CORES
        for k in range(1, NZ):
            dst = val_all.at[own_part(i, (z + NZ - k) % NZ)]
            wait_for(dst, vs_send.at[i, 3 + k], vs_recv.at[i, 3 + k], along_z(NZ - k))
        src = val_all.at[pl.ds(pl.multiple_of(STARTS[i] + core * half, half), half)]
        copy_to(src, src, vs_send.at[i, 7], vs_recv.at[i, 7], sibling)

    def send_first():
        for k in range(1, NX):
            src, dst = g_one_out.at[(x + k) % NX], g_one_in.at[k]
            copy_to(src, dst, g_send.at[0, k], g_recv.at[0, k], along_x(k))

    def send_second():
        for k in range(1, NY):
            src, dst = g_two_out.at[(y + k) % NY], g_two_in.at[k]
            copy_to(src, dst, g_send.at[1, k], g_recv.at[1, k], along_y(k))

    def add_gradient(i):
        start, size = STARTS[i], SIZES[i]
        half = size // CORES
        dst = val_all.at[pl.ds(pl.multiple_of(start + other * half, half), half)]
        wait_for(dst, vs_send.at[i, 7], vs_recv.at[i, 7], sibling)
        here = pl.ds(start, size)
        requests = accept.shape[1]
        row = lax.broadcasted_iota(jnp.int32, (size, requests), 0) + start
        request = lax.broadcasted_iota(jnp.int32, (size, requests), 1)
        taken = jnp.sum(
            jnp.where(row // SPEC == request, accept[...], 0).astype(F32), axis=1, keepdims=True
        )
        order = (lax.broadcasted_iota(jnp.int32, (size, 1), 0) % SPEC).astype(F32)
        weight = jnp.where(order < taken, scales[here, :1], 0.0)
        errors = weight * (val_all[here, :].astype(F32) - tgt_own[here, :].astype(F32))
        errors = errors.T.astype(BF16)
        for part_of, send in ((0, send_first), (1, send_second)):
            there = pl.ds(part_of * side, side)
            product = jnp.dot(errors, u_all[here, there], preferred_element_type=F32)
            if i > 0:
                product = product + g_sum[:, there]
            g_sum[:, there] = product
            if i == CHUNKS - 1:
                for yy in range(NY):
                    for xx in range(NX):
                        first = (yy * NX + xx) * own_rows
                        piece = product[first : first + own_rows].astype(BF16)
                        if part_of == 0:
                            g_one_out[xx, yy] = piece
                        else:
                            g_two_out[yy, xx] = piece
                send()

    for it in range(CHUNKS + 5):
        for stage, lag in (
            (pass_on, 0),
            (pass_far, 1),
            (add_pair, 2),
            (finish_values, 3),
            (pass_values, 4),
            (add_gradient, 5),
            (multiply, 1),
        ):
            if 0 <= it - lag < CHUNKS:
                stage(it - lag)

    slot = lax.broadcasted_iota(jnp.int32, (capacity, rows), 0)
    for j in range(2):
        pick = (slot + pred_to(j)[0] * capacity == spot[...]).astype(F32).astype(BF16)
        p_out[j] = jnp.dot(pick, val_all[...], preferred_element_type=F32).astype(BF16)

    def pred_copy(j):
        return pltpu.make_async_remote_copy(
            src_ref=p_out.at[j],
            dst_ref=pred.at[pl.ds(pl.multiple_of((g % 2) * capacity, capacity), capacity)],
            send_sem=p_send.at[j],
            recv_sem=p_recv.at[g % 2],
            device_id=pred_to(j),
            device_id_type=MESH,
        )

    def pred_local(j):
        return pltpu.make_async_copy(
            p_out.at[j],
            pred.at[pl.ds(pl.multiple_of((g % 2) * capacity, capacity), capacity)],
            p_send.at[j],
        )

    for j in range(2):

        @pl.when(is_self(pred_to(j)))
        def _():
            pred_local(j).start()

        @pl.when(jnp.logical_not(is_self(pred_to(j))))
        def _():
            pred_copy(j).start()

    for k in range(1, NX):
        wait_for(g_one_in.at[k], g_send.at[0, k], g_recv.at[0, k], along_x(NX - k))
    for yy in range(NY):
        mine = pl.ds(pl.multiple_of((yy * NX + x) * own_rows, own_rows), own_rows)
        total = g_sum[mine, :side]
        for k in range(1, NX):
            total = total + g_one_in[k, yy].astype(F32)
        h_one[yy] = total
        h_one_out[yy] = total.astype(BF16)
    for k in range(1, NY):
        src, dst = h_one_out.at[(y + k) % NY], h_one_in.at[k]
        copy_to(src, dst, g_send.at[2, k], g_recv.at[2, k], along_y(k))
    for k in range(1, NY):
        wait_for(g_two_in.at[k], g_send.at[1, k], g_recv.at[1, k], along_y(NY - k))
    for xx in range(NX):
        mine = pl.ds(pl.multiple_of((y * NX + xx) * own_rows, own_rows), own_rows)
        total = g_sum[mine, side:]
        for k in range(1, NY):
            total = total + g_two_in[k, xx].astype(F32)
        h_two[xx] = total
        h_two_out[xx] = total.astype(BF16)
    for k in range(1, NX):
        src, dst = h_two_out.at[(x + k) % NX], h_two_in.at[k]
        copy_to(src, dst, g_send.at[3, k], g_recv.at[3, k], along_x(k))
    norm = 1.0 / math.sqrt(rows * groups)
    total = h_one[y]
    for k in range(1, NY):
        wait_for(h_one_in.at[k], g_send.at[2, k], g_recv.at[2, k], along_y(NY - k))
        total = total + h_one_in[k].astype(F32)
    grad[:, :side] = total * norm
    total = h_two[x]
    for k in range(1, NX):
        wait_for(h_two_in.at[k], g_send.at[3, k], g_recv.at[3, k], along_x(NX - k))
        total = total + h_two_in[k].astype(F32)
    grad[:, side:] = total * norm

    for j in range(2):

        @pl.when(is_self(pred_to(j)))
        def _():
            pred_local(j).wait()

        @pl.when(jnp.logical_not(is_self(pred_to(j))))
        def _():
            pred_copy(j).wait_send()

        @pl.when(jnp.logical_not(is_self(pred_from(j))))
        def _():
            dst = pred.at[pl.ds(j * capacity, capacity)]
            wait_for(dst, p_send.at[j], p_recv.at[j], pred_from(j))

    for copy in sends:
        copy.wait_send()


def local(
    attn_out,
    o_proj,
    residual,
    norm_gain,
    dest_group,
    accept_count,
    target_values,
    master,
    moment_one,
    moment_two,
):
    groups = lax.axis_size("grp")
    rows, width = attn_out.shape
    depth, cols = o_proj.shape
    kvw = target_values.shape[1]
    own_rows = master.shape[0]
    capacity = 2 * rows // groups
    side = cols // 2
    largest = max(SIZES)
    any_spec = pl.BlockSpec(memory_space=pl.ANY)
    vmem_spec = pl.BlockSpec(memory_space=pltpu.VMEM)
    vmem = pltpu.VMEM
    dma = pltpu.SemaphoreType.DMA
    pred, grad = pl.pallas_call(
        kernel,
        out_shape=(
            jax.ShapeDtypeStruct((2 * capacity, kvw), BF16),
            jax.ShapeDtypeStruct((own_rows, cols), F32),
        ),
        in_specs=[any_spec, any_spec, any_spec, vmem_spec, vmem_spec, vmem_spec, any_spec, any_spec],
        out_specs=(any_spec, vmem_spec),
        scratch_shapes=[
            vmem((rows, depth), BF16),
            vmem((depth, cols), BF16),
            vmem((rows, cols), BF16),
            vmem((rows, kvw), BF16),
            vmem((own_rows, cols), F32),
            vmem((kvw, cols), BF16),
            vmem((rows, cols), BF16),
            vmem((SIZES[-1], cols), F32),
            vmem((rows, kvw), BF16),
            vmem((rows // CORES, kvw), BF16),
            vmem((rows // CORES, kvw), BF16),
            vmem((NZ, rows // (CORES * NZ), kvw), BF16),
            vmem((rows, kvw), BF16),
            vmem((CHUNKS, 8, largest), F32),
            vmem((CHUNKS, 8, largest), F32),
            vmem((CHUNKS, 8, largest), F32),
            vmem((CHUNKS, NZ, 8, largest), F32),
            vmem((rows, LANES), F32),
            vmem((kvw, cols), F32),
            vmem((NX, NY, own_rows, side), BF16),
            vmem((NY, NX, own_rows, side), BF16),
            vmem((NX, NY, own_rows, side), BF16),
            vmem((NY, NX, own_rows, side), BF16),
            vmem((NY, own_rows, side), F32),
            vmem((NX, own_rows, side), F32),
            vmem((NY, own_rows, side), BF16),
            vmem((NX, own_rows, side), BF16),
            vmem((NY, own_rows, side), BF16),
            vmem((NX, own_rows, side), BF16),
            vmem((2, capacity, kvw), BF16),
            vmem((1, rows), jnp.int32),
            dma((12,)),
            dma((CHUNKS, 8)),
            dma((CHUNKS, 8)),
            dma((CHUNKS, 8)),
            dma((CHUNKS, 8)),
            dma((CHUNKS, NZ)),
            dma((CHUNKS, NZ)),
            dma((2, NX)),
            dma((2, NX)),
            dma((4, NX)),
            dma((4, NX)),
            dma((2,)),
            dma((2,)),
        ],
        compiler_params=pltpu.CompilerParams(
            collective_id=0, has_side_effects=True, vmem_limit_bytes=56 * 2**20
        ),
        cost_estimate=pl.CostEstimate(
            flops=2 * rows * cols * (depth + 2 * kvw),
            bytes_accessed=2 * (depth * cols + rows * (cols + width + kvw)),
            transcendentals=0,
        ),
        name="step",
    )(
        attn_out,
        o_proj,
        residual,
        norm_gain.reshape(1, cols),
        dest_group.reshape(1, rows),
        accept_count.reshape(1, rows // SPEC),
        target_values,
        master,
    )
    own = jax.ShapeDtypeStruct((own_rows, cols), F32)
    return pl.pallas_call(
        finish_kernel,
        out_shape=(jax.ShapeDtypeStruct((2 * capacity, kvw), BF16), own, own, own),
        in_specs=[vmem_spec] * 5,
        out_specs=(vmem_spec,) * 4,
        cost_estimate=pl.CostEstimate(
            flops=16 * own_rows * cols, bytes_accessed=28 * own_rows * cols, transcendentals=0
        ),
        name="finish",
    )(pred, grad, master, moment_one, moment_two)


def solution(mesh):
    in_specs = (
        P("grp", "tp"),
        P(None, "tp"),
        P("grp", "tp"),
        P("tp"),
        P("grp", None),
        P("grp"),
        P("grp", None),
        P("grp", "tp"),
        P("grp", "tp"),
        P("grp", "tp"),
    )
    out_specs = (P(("grp", "tp"), None), P("grp", "tp"), P("grp", "tp"), P("grp", "tp"))
    return jax.shard_map(local, mesh=mesh, in_specs=in_specs, out_specs=out_specs, check_vma=False)
```

```python
import functools
import math

import jax
import jax.numpy as jnp
from jax import lax
from jax.experimental import pallas as pl
from jax.experimental.pallas import tpu as pltpu
from jax.sharding import PartitionSpec as P

D = 8192
SPEC = 8


norm_eps = 1e-06
beta_one = 0.9
beta_two = 0.95
adam_eps = 1e-08
learn_rate = 0.01
decay_rate = 0.1
step_count = 10

MESH = pl.DeviceIdType.MESH
F32 = jnp.float32
BF16 = jnp.bfloat16

NX, NY, NZ, CORES = 4, 4, 4, 2
SIZES = (384, 384, 256)
STARTS = tuple(sum(SIZES[:i]) for i in range(len(SIZES)))
CHUNKS = len(SIZES)
LANES = 128
TILE = 256
OWN, UP, DOWN, FAR = range(4)


def adam_update(master, moment_one, moment_two, gradient):
    first_moment = beta_one * moment_one + (1.0 - beta_one) * gradient
    second_moment = beta_two * moment_two + (1.0 - beta_two) * gradient * gradient
    update = (
        first_moment
        / (1.0 - beta_one**step_count)
        / (jnp.sqrt(second_moment / (1.0 - beta_two**step_count)) + adam_eps)
    )
    return (master - learn_rate * (update + decay_rate * master), first_moment, second_moment)


def finish_kernel(pred, grad, master, one, two, pred_out, master_out, one_out, two_out):
    pred_out[...] = pred[...]
    master_out[...], one_out[...], two_out[...] = adam_update(
        master[...], one[...], two[...], grad[...]
    )


def kernel(
    attn,
    o_proj,
    residual,
    gain,
    dest,
    accept,
    target,
    master,
    pred,
    grad,
    a_all,
    w_own,
    res_own,
    tgt_own,
    mst_own,
    mst_all,
    u_all,
    near,
    part,
    pair_in,
    pair_sum,
    z_in,
    val_all,
    sq_out,
    sq_pair,
    sq_sum,
    sq_z,
    scales,
    live,
    g_sum,
    g_one_out,
    g_two_out,
    g_one_in,
    g_two_in,
    h_one,
    h_two,
    h_one_out,
    h_two_out,
    h_one_in,
    h_two_in,
    p_out,
    spot,
    load_sem,
    ag_send,
    ag_recv,
    vs_send,
    vs_recv,
    sq_send,
    sq_recv,
    m_send,
    m_recv,
    g_send,
    g_recv,
    p_send,
    p_recv,
):
    rows, width = attn.shape
    cols = o_proj.shape[1]
    kvw = target.shape[1]
    groups = NX * NY
    own_rows = kvw // groups
    side = cols // 2
    capacity = 2 * rows // groups
    g, t = lax.axis_index("grp"), lax.axis_index("tp")
    z, core = t // CORES, t % CORES
    y, x = g // NX, g % NX
    other = 1 - core

    def along_z(k):
        return (g, ((z + k) % NZ) * CORES + core)

    def along_x(k):
        return (y * NX + (x + k) % NX, t)

    def along_y(k):
        return (((y + k) % NY) * NX + x, t)

    up, down, far = along_z(1), along_z(NZ - 1), along_z(2)
    sibling = (g, z * CORES + other)

    def pred_to(j):
        turn = z + x if j == 0 else 2 * NY - z - x
        return ((y + turn) % NY) * NX + 2 * core + j, g // 2

    def pred_from(j):
        source = 2 * t + j
        source_y, source_x = source // NX, source % NX
        odd = x % 2
        turn = (y - source_y + NY) * (1 - odd) + (source_y - y + NY) * odd
        return source, ((turn - source_x + 2 * NZ) % NZ) * CORES + x // 2

    def is_self(device):
        return jnp.logical_and(device[0] == g, device[1] == t)

    sends = []

    def copy_to(src, dst, send_sem, recv_sem, device):
        copy = pltpu.make_async_remote_copy(
            src_ref=src,
            dst_ref=dst,
            send_sem=send_sem,
            recv_sem=recv_sem,
            device_id=device,
            device_id_type=MESH,
        )
        copy.start()
        sends.append(copy)

    def wait_for(dst, send_sem, recv_sem, device):
        pltpu.make_async_remote_copy(
            src_ref=dst,
            dst_ref=dst,
            send_sem=send_sem,
            recv_sem=recv_sem,
            device_id=device,
            device_id_type=MESH,
        ).wait_recv()

    def place(which, cc):
        return pl.ds(pl.multiple_of((which * CORES + cc) * width, width), width)

    def block(which, cc, start, size):
        return a_all.at[pl.ds(start, size), place(which, cc)]

    loads = [
        pltpu.make_async_copy(master, mst_own, load_sem.at[0]),
        pltpu.make_async_copy(attn, block(OWN, core, 0, rows), load_sem.at[1]),
        pltpu.make_async_copy(residual, res_own, load_sem.at[2]),
        pltpu.make_async_copy(target, tgt_own, load_sem.at[3]),
    ]
    for which, step in ((OWN, 0), (UP, 1), (DOWN, NZ - 1), (FAR, 2)):
        for cc in range(CORES):
            first = ((z + step) % NZ * CORES + cc) * width
            loads.append(
                pltpu.make_async_copy(
                    o_proj.at[pl.ds(pl.multiple_of(first, width), width)],
                    w_own.at[place(which, cc)],
                    load_sem.at[4 + which * CORES + cc],
                )
            )
    for load in loads:
        load.start()

    barrier = pltpu.get_barrier_semaphore()

    def greet(device):
        pl.semaphore_signal(barrier, inc=1, device_id=device, device_id_type=MESH)

    for k in range(1, NZ):
        greet(along_z(k))
        greet(along_x(k))
        greet(along_y(k))
    greet(sibling)
    expected = jnp.int32(3 * (NZ - 1) + 1)
    for j in range(2):

        @pl.when(jnp.logical_not(is_self(pred_from(j))))
        def _():
            greet(pred_from(j))

        expected = expected + 1 - is_self(pred_to(j)).astype(jnp.int32)
    pl.semaphore_wait(barrier, expected)

    def send_own(i):
        start, size = STARTS[i], SIZES[i]
        src = attn.at[pl.ds(start, size)]
        copy_to(src, block(DOWN, core, start, size), ag_send.at[i, 0], ag_recv.at[i, 0], up)
        copy_to(src, block(UP, core, start, size), ag_send.at[i, 1], ag_recv.at[i, 1], down)
        copy_to(src, block(OWN, core, start, size), ag_send.at[i, 2], ag_recv.at[i, 2], sibling)

    send_own(0)
    send_own(1)

    def mst_rows(first, count):
        return mst_all.at[pl.ds(pl.multiple_of(first * own_rows, own_rows), count * own_rows)]

    loads[0].wait()
    mst_rows(g, 1)[...] = mst_own[...].astype(BF16)
    for k in range(1, NX):
        copy_to(mst_rows(g, 1), mst_rows(g, 1), m_send.at[0, k], m_recv.at[0, k], along_x(k))

    for n in range(rows // TILE):
        here = pl.ds(n * TILE, TILE)
        kinds = lax.broadcasted_iota(jnp.int32, (groups, rows), 0)
        onehot = (kinds == dest[...]).astype(F32).astype(BF16)
        earlier_rows = lax.broadcasted_iota(jnp.int32, (rows, TILE), 0)
        these_rows = lax.broadcasted_iota(jnp.int32, (rows, TILE), 1) + n * TILE
        before = (earlier_rows < these_rows).astype(F32).astype(BF16)
        earlier = jnp.dot(onehot, before, preferred_element_type=F32)
        dest_here = dest[:, here]
        mine = lax.broadcasted_iota(jnp.int32, (groups, TILE), 0) == dest_here
        rank = jnp.sum(jnp.where(mine, earlier, 0.0), axis=0, keepdims=True)
        spot[:, here] = dest_here * capacity + rank.astype(jnp.int32)

    requests = accept.shape[1]
    for n in range(rows // TILE):
        here = pl.ds(n * TILE, TILE)
        row = lax.broadcasted_iota(jnp.int32, (TILE, requests), 0) + n * TILE
        request = lax.broadcasted_iota(jnp.int32, (TILE, requests), 1)
        taken = jnp.sum(
            jnp.where(row // SPEC == request, accept[...], 0).astype(F32), axis=1, keepdims=True
        )
        order = (lax.broadcasted_iota(jnp.int32, (TILE, LANES), 0) % SPEC).astype(F32)
        live[here, :] = jnp.where(order < taken, 1.0, 0.0)

    for k in range(1, NX):
        source = along_x(NX - k)
        wait_for(mst_rows(source[0], 1), m_send.at[0, k], m_recv.at[0, k], source)
    for k in range(1, NY):
        src = mst_rows(y * NX, NX)
        copy_to(src, src, m_send.at[1, k], m_recv.at[1, k], along_y(k))

    def pass_on(i):
        start, size = STARTS[i], SIZES[i]
        part_size = size // 2
        src = block(DOWN, core, start, size)
        wait_for(src, ag_send.at[i, 0], ag_recv.at[i, 0], down)
        copy_to(
            block(DOWN, core, start, part_size),
            block(FAR, core, start, part_size),
            ag_send.at[i, 3],
            ag_recv.at[i, 3],
            up,
        )
        copy_to(src, src, ag_send.at[i, 4], ag_recv.at[i, 4], sibling)
        src = block(UP, core, start, size)
        wait_for(src, ag_send.at[i, 1], ag_recv.at[i, 1], up)
        copy_to(
            block(UP, core, start + part_size, part_size),
            block(FAR, core, start + part_size, part_size),
            ag_send.at[i, 5],
            ag_recv.at[i, 5],
            down,
        )
        copy_to(src, src, ag_send.at[i, 6], ag_recv.at[i, 6], sibling)
        if i + 2 < CHUNKS:
            send_own(i + 2)

    def pass_far(i):
        start, size = STARTS[i], SIZES[i]
        part_size = size // 2
        wait_for(
            block(FAR, core, start, part_size), ag_send.at[i, 3], ag_recv.at[i, 3], down
        )
        wait_for(
            block(FAR, core, start + part_size, part_size), ag_send.at[i, 5], ag_recv.at[i, 5], up
        )
        src = block(FAR, core, start, size)
        copy_to(src, src, ag_send.at[i, 7], ag_recv.at[i, 7], sibling)

    depth = FAR * CORES * width

    def multiply_near(i):
        start, size = STARTS[i], SIZES[i]
        here = pl.ds(start, size)
        for which, sem in ((OWN, 2), (DOWN, 4), (UP, 6)):
            wait_for(block(which, other, start, size), ag_send.at[i, sem], ag_recv.at[i, sem], sibling)
        if i == 0:
            for load in loads[1:]:
                load.wait()

        def columns(n, carry):
            there = pl.ds(pl.multiple_of(n * TILE, TILE), TILE)
            near[i % 2, :size, there] = jnp.dot(
                a_all[here, :depth], w_own[:depth, there], preferred_element_type=F32
            )
            return carry

        lax.fori_loop(0, cols // TILE, columns, 0, unroll=True)

    def multiply_far(i):
        start, size = STARTS[i], SIZES[i]
        here = pl.ds(start, size)
        wait_for(block(FAR, other, start, size), ag_send.at[i, 7], ag_recv.at[i, 7], sibling)

        def columns(n, squares):
            there = pl.ds(pl.multiple_of(n * TILE, TILE), TILE)
            hidden = near[i % 2, :size, there] + jnp.dot(
                a_all[here, depth:], w_own[depth:, there], preferred_element_type=F32
            )
            hidden = hidden + res_own[here, there].astype(F32)
            u_all[here, there] = (hidden * gain[:, there]).astype(BF16)
            squared = hidden * hidden
            return squares + squared[:, :LANES] + squared[:, LANES:]

        squares = lax.fori_loop(0, cols // TILE, columns, jnp.zeros((size, LANES), F32), unroll=True)
        total = jnp.sum(squares.T, axis=0, keepdims=True)
        sq_out[i, :, :size] = jnp.broadcast_to(total, (8, size))
        copy_to(sq_out.at[i], sq_pair.at[i], sq_send.at[i, 0], sq_recv.at[i, 0], sibling)
        if i == 0:
            for k in range(1, NY):
                source = (y + NY - k) % NY
                wait_for(
                    mst_rows(source * NX, NX), m_send.at[1, k], m_recv.at[1, k], along_y(NY - k)
                )
        part[here, :] = lax.dot_general(
            u_all[here, :],
            mst_all[...],
            (((1,), (1,)), ((), ())),
            preferred_element_type=F32,
        ).astype(BF16)
        half = size // CORES
        src = part.at[pl.ds(pl.multiple_of(start + other * half, half), half)]
        dst = pair_in.at[pl.ds(start // CORES, half)]
        copy_to(src, dst, vs_send.at[i, 0], vs_recv.at[i, 0], sibling)

    def add_pair(i):
        start, size = STARTS[i], SIZES[i]
        half = size // CORES
        sub = half // NZ
        first = start // CORES
        wait_for(sq_pair.at[i], sq_send.at[i, 0], sq_recv.at[i, 0], sibling)
        sq_sum[i] = sq_out[i] + sq_pair[i]
        for k in range(1, NZ):
            copy_to(sq_sum.at[i], sq_z.at[i, k], sq_send.at[i, k], sq_recv.at[i, k], along_z(k))
        here = pl.ds(first, half)
        wait_for(pair_in.at[here], vs_send.at[i, 0], vs_recv.at[i, 0], sibling)
        mine = pl.ds(pl.multiple_of(start + core * half, half), half)
        pair_sum[here, :] = (part[mine, :].astype(F32) + pair_in[here, :].astype(F32)).astype(BF16)
        for k in range(1, NZ):
            src = pair_sum.at[pl.ds(pl.multiple_of(first + (z + k) % NZ * sub, sub), sub)]
            dst = z_in.at[k, pl.ds(start // (CORES * NZ), sub)]
            copy_to(src, dst, vs_send.at[i, k], vs_recv.at[i, k], along_z(k))

    def own_part(i, zz):
        sub = SIZES[i] // (CORES * NZ)
        return pl.ds(pl.multiple_of(STARTS[i] + (core * NZ + zz) * sub, sub), sub)

    def finish_values(i):
        start, size = STARTS[i], SIZES[i]
        sub = size // (CORES * NZ)
        total = sq_sum[i]
        for k in range(1, NZ):
            wait_for(sq_z.at[i, k], sq_send.at[i, k], sq_recv.at[i, k], along_z(NZ - k))
            total = total + sq_z[i, k]
        scale = lax.rsqrt(total[:1, :size] / D + norm_eps)
        scales[pl.ds(start, size), :] = jnp.broadcast_to(scale, (LANES, size)).T
        mine = pl.ds(pl.multiple_of(start // CORES + z * sub, sub), sub)
        there = pl.ds(start // (CORES * NZ), sub)
        values = pair_sum[mine, :].astype(F32)
        for k in range(1, NZ):
            wait_for(z_in.at[k, there], vs_send.at[i, k], vs_recv.at[i, k], along_z(NZ - k))
            values = values + z_in[k, there, :].astype(F32)
        here = own_part(i, z)
        val_all[here, :] = (values * scales[here, :1]).astype(BF16)
        src = val_all.at[here]
        for k in range(1, NZ):
            copy_to(src, src, vs_send.at[i, 3 + k], vs_recv.at[i, 3 + k], along_z(k))

    def pass_values(i):
        half = SIZES[i] // CORES
        for k in range(1, NZ):
            dst = val_all.at[own_part(i, (z + NZ - k) % NZ)]
            wait_for(dst, vs_send.at[i, 3 + k], vs_recv.at[i, 3 + k], along_z(NZ - k))
        src = val_all.at[pl.ds(pl.multiple_of(STARTS[i] + core * half, half), half)]
        copy_to(src, src, vs_send.at[i, 7], vs_recv.at[i, 7], sibling)

    def send_first():
        for k in range(1, NX):
            src, dst = g_one_out.at[(x + k) % NX], g_one_in.at[k]
            copy_to(src, dst, g_send.at[0, k], g_recv.at[0, k], along_x(k))

    def send_second():
        for k in range(1, NY):
            src, dst = g_two_out.at[(y + k) % NY], g_two_in.at[k]
            copy_to(src, dst, g_send.at[1, k], g_recv.at[1, k], along_y(k))

    def add_gradient(i):
        start, size = STARTS[i], SIZES[i]
        half = size // CORES
        dst = val_all.at[pl.ds(pl.multiple_of(start + other * half, half), half)]
        wait_for(dst, vs_send.at[i, 7], vs_recv.at[i, 7], sibling)
        here = pl.ds(start, size)
        weight = live[here, :1] * scales[here, :1]
        errors = weight * (val_all[here, :].astype(F32) - tgt_own[here, :].astype(F32))
        errors = errors.T.astype(BF16)
        for part_of, send in ((0, send_first), (1, send_second)):
            there = pl.ds(part_of * side, side)
            product = jnp.dot(errors, u_all[here, there], preferred_element_type=F32)
            if i > 0:
                product = product + g_sum[:, there]
            g_sum[:, there] = product
            if i == CHUNKS - 1:
                for yy in range(NY):
                    for xx in range(NX):
                        first = (yy * NX + xx) * own_rows
                        piece = product[first : first + own_rows].astype(BF16)
                        if part_of == 0:
                            g_one_out[xx, yy] = piece
                        else:
                            g_two_out[yy, xx] = piece
                send()

    for it in range(CHUNKS + 5):
        for stage, lag in (
            (pass_on, 0),
            (add_pair, 2),
            (finish_values, 3),
            (pass_values, 4),
            (multiply_near, 0),
            (pass_far, 1),
            (multiply_far, 1),
            (add_gradient, 5),
        ):
            if 0 <= it - lag < CHUNKS:
                stage(it - lag)

    slot = lax.broadcasted_iota(jnp.int32, (capacity, rows), 0)
    for j in range(2):
        pick = (slot + pred_to(j)[0] * capacity == spot[...]).astype(F32).astype(BF16)
        p_out[j] = jnp.dot(pick, val_all[...], preferred_element_type=F32).astype(BF16)

    def pred_copy(j):
        return pltpu.make_async_remote_copy(
            src_ref=p_out.at[j],
            dst_ref=pred.at[pl.ds(pl.multiple_of((g % 2) * capacity, capacity), capacity)],
            send_sem=p_send.at[j],
            recv_sem=p_recv.at[g % 2],
            device_id=pred_to(j),
            device_id_type=MESH,
        )

    def pred_local(j):
        return pltpu.make_async_copy(
            p_out.at[j],
            pred.at[pl.ds(pl.multiple_of((g % 2) * capacity, capacity), capacity)],
            p_send.at[j],
        )

    for j in range(2):

        @pl.when(is_self(pred_to(j)))
        def _():
            pred_local(j).start()

        @pl.when(jnp.logical_not(is_self(pred_to(j))))
        def _():
            pred_copy(j).start()

    early = len(sends) - NX - NY + 2
    for copy in sends[:early]:
        copy.wait_send()
    del sends[:early]

    for k in range(1, NX):
        wait_for(g_one_in.at[k], g_send.at[0, k], g_recv.at[0, k], along_x(NX - k))
    for yy in range(NY):
        mine = pl.ds(pl.multiple_of((yy * NX + x) * own_rows, own_rows), own_rows)
        total = g_sum[mine, :side]
        for k in range(1, NX):
            total = total + g_one_in[k, yy].astype(F32)
        h_one[yy] = total
        h_one_out[yy] = total.astype(BF16)
    for k in range(1, NY):
        src, dst = h_one_out.at[(y + k) % NY], h_one_in.at[k]
        copy_to(src, dst, g_send.at[2, k], g_recv.at[2, k], along_y(k))
    for k in range(1, NY):
        wait_for(g_two_in.at[k], g_send.at[1, k], g_recv.at[1, k], along_y(NY - k))
    for xx in range(NX):
        mine = pl.ds(pl.multiple_of((y * NX + xx) * own_rows, own_rows), own_rows)
        total = g_sum[mine, side:]
        for k in range(1, NY):
            total = total + g_two_in[k, xx].astype(F32)
        h_two[xx] = total
        h_two_out[xx] = total.astype(BF16)
    for k in range(1, NX):
        src, dst = h_two_out.at[(x + k) % NX], h_two_in.at[k]
        copy_to(src, dst, g_send.at[3, k], g_recv.at[3, k], along_x(k))
    norm = 1.0 / math.sqrt(rows * groups)
    total = h_one[y]
    for k in range(1, NY):
        wait_for(h_one_in.at[k], g_send.at[2, k], g_recv.at[2, k], along_y(NY - k))
        total = total + h_one_in[k].astype(F32)
    grad[:, :side] = total * norm
    total = h_two[x]
    for k in range(1, NX):
        wait_for(h_two_in.at[k], g_send.at[3, k], g_recv.at[3, k], along_x(NX - k))
        total = total + h_two_in[k].astype(F32)
    grad[:, side:] = total * norm

    for j in range(2):

        @pl.when(is_self(pred_to(j)))
        def _():
            pred_local(j).wait()

        @pl.when(jnp.logical_not(is_self(pred_to(j))))
        def _():
            pred_copy(j).wait_send()

        @pl.when(jnp.logical_not(is_self(pred_from(j))))
        def _():
            dst = pred.at[pl.ds(j * capacity, capacity)]
            wait_for(dst, p_send.at[j], p_recv.at[j], pred_from(j))

    for copy in sends:
        copy.wait_send()


def local(
    attn_out,
    o_proj,
    residual,
    norm_gain,
    dest_group,
    accept_count,
    target_values,
    master,
    moment_one,
    moment_two,
):
    groups = lax.axis_size("grp")
    rows, width = attn_out.shape
    depth, cols = o_proj.shape
    kvw = target_values.shape[1]
    own_rows = master.shape[0]
    capacity = 2 * rows // groups
    side = cols // 2
    largest = max(SIZES)
    any_spec = pl.BlockSpec(memory_space=pl.ANY)
    vmem_spec = pl.BlockSpec(memory_space=pltpu.VMEM)
    vmem = pltpu.VMEM
    dma = pltpu.SemaphoreType.DMA
    pred, grad = pl.pallas_call(
        kernel,
        out_shape=(
            jax.ShapeDtypeStruct((2 * capacity, kvw), BF16),
            jax.ShapeDtypeStruct((own_rows, cols), F32),
        ),
        in_specs=[any_spec, any_spec, any_spec, vmem_spec, vmem_spec, vmem_spec, any_spec, any_spec],
        out_specs=(any_spec, vmem_spec),
        scratch_shapes=[
            vmem((rows, depth), BF16),
            vmem((depth, cols), BF16),
            vmem((rows, cols), BF16),
            vmem((rows, kvw), BF16),
            vmem((own_rows, cols), F32),
            vmem((kvw, cols), BF16),
            vmem((rows, cols), BF16),
            vmem((2, largest, cols), F32),
            vmem((rows, kvw), BF16),
            vmem((rows // CORES, kvw), BF16),
            vmem((rows // CORES, kvw), BF16),
            vmem((NZ, rows // (CORES * NZ), kvw), BF16),
            vmem((rows, kvw), BF16),
            vmem((CHUNKS, 8, largest), F32),
            vmem((CHUNKS, 8, largest), F32),
            vmem((CHUNKS, 8, largest), F32),
            vmem((CHUNKS, NZ, 8, largest), F32),
            vmem((rows, LANES), F32),
            vmem((rows, LANES), F32),
            vmem((kvw, cols), F32),
            vmem((NX, NY, own_rows, side), BF16),
            vmem((NY, NX, own_rows, side), BF16),
            vmem((NX, NY, own_rows, side), BF16),
            vmem((NY, NX, own_rows, side), BF16),
            vmem((NY, own_rows, side), F32),
            vmem((NX, own_rows, side), F32),
            vmem((NY, own_rows, side), BF16),
            vmem((NX, own_rows, side), BF16),
            vmem((NY, own_rows, side), BF16),
            vmem((NX, own_rows, side), BF16),
            vmem((2, capacity, kvw), BF16),
            vmem((1, rows), jnp.int32),
            dma((12,)),
            dma((CHUNKS, 8)),
            dma((CHUNKS, 8)),
            dma((CHUNKS, 8)),
            dma((CHUNKS, 8)),
            dma((CHUNKS, NZ)),
            dma((CHUNKS, NZ)),
            dma((2, NX)),
            dma((2, NX)),
            dma((4, NX)),
            dma((4, NX)),
            dma((2,)),
            dma((2,)),
        ],
        compiler_params=pltpu.CompilerParams(
            collective_id=0, has_side_effects=True, vmem_limit_bytes=56 * 2**20
        ),
        cost_estimate=pl.CostEstimate(
            flops=2 * rows * cols * (depth + 2 * kvw),
            bytes_accessed=2 * (depth * cols + rows * (cols + width + kvw)),
            transcendentals=0,
        ),
        name="step",
    )(
        attn_out,
        o_proj,
        residual,
        norm_gain.reshape(1, cols),
        dest_group.reshape(1, rows),
        accept_count.reshape(1, rows // SPEC),
        target_values,
        master,
    )
    own = jax.ShapeDtypeStruct((own_rows, cols), F32)
    return pl.pallas_call(
        finish_kernel,
        out_shape=(jax.ShapeDtypeStruct((2 * capacity, kvw), BF16), own, own, own),
        in_specs=[vmem_spec] * 5,
        out_specs=(vmem_spec,) * 4,
        cost_estimate=pl.CostEstimate(
            flops=16 * own_rows * cols, bytes_accessed=28 * own_rows * cols, transcendentals=0
        ),
        name="finish",
    )(pred, grad, master, moment_one, moment_two)


def solution(mesh):
    in_specs = (
        P("grp", "tp"),
        P(None, "tp"),
        P("grp", "tp"),
        P("tp"),
        P("grp", None),
        P("grp"),
        P("grp", None),
        P("grp", "tp"),
        P("grp", "tp"),
        P("grp", "tp"),
    )
    out_specs = (P(("grp", "tp"), None), P("grp", "tp"), P("grp", "tp"), P("grp", "tp"))
    return jax.shard_map(local, mesh=mesh, in_specs=in_specs, out_specs=out_specs, check_vma=False)
```

```python
import functools
import math

import jax
import jax.numpy as jnp
from jax import lax
from jax.experimental import pallas as pl
from jax.experimental.pallas import tpu as pltpu
from jax.sharding import PartitionSpec as P

D = 8192
SPEC = 8


norm_eps = 1e-06
beta_one = 0.9
beta_two = 0.95
adam_eps = 1e-08
learn_rate = 0.01
decay_rate = 0.1
step_count = 10

MESH = pl.DeviceIdType.MESH
F32 = jnp.float32
BF16 = jnp.bfloat16

NX, NY, NZ, CORES = 4, 4, 4, 2
SIZES = (384, 384, 256)
STARTS = tuple(sum(SIZES[:i]) for i in range(len(SIZES)))
CHUNKS = len(SIZES)
LANES = 128
TILE = 256
OWN, UP, DOWN, FAR = range(4)


def adam_update(master, moment_one, moment_two, gradient):
    first_moment = beta_one * moment_one + (1.0 - beta_one) * gradient
    second_moment = beta_two * moment_two + (1.0 - beta_two) * gradient * gradient
    update = (
        first_moment
        / (1.0 - beta_one**step_count)
        / (jnp.sqrt(second_moment / (1.0 - beta_two**step_count)) + adam_eps)
    )
    return (master - learn_rate * (update + decay_rate * master), first_moment, second_moment)


def finish_kernel(pred, grad, master, one, two, pred_out, master_out, one_out, two_out):
    pred_out[...] = pred[...]
    master_out[...], one_out[...], two_out[...] = adam_update(
        master[...], one[...], two[...], grad[...]
    )


def kernel(
    attn,
    o_proj,
    residual,
    gain,
    dest,
    accept,
    target,
    master,
    pred,
    grad,
    a_all,
    w_own,
    res_own,
    tgt_own,
    mst_own,
    mst_all,
    u_all,
    near,
    part,
    pair_in,
    pair_sum,
    z_in,
    val_all,
    sq_out,
    sq_pair,
    sq_sum,
    sq_z,
    scales,
    live,
    g_sum,
    g_one_out,
    g_two_out,
    g_one_in,
    g_two_in,
    h_one,
    h_two,
    h_one_out,
    h_two_out,
    h_one_in,
    h_two_in,
    p_out,
    spot,
    load_sem,
    ag_send,
    ag_recv,
    vs_send,
    vs_recv,
    sq_send,
    sq_recv,
    m_send,
    m_recv,
    g_send,
    g_recv,
    p_send,
    p_recv,
):
    rows, width = attn.shape
    cols = o_proj.shape[1]
    kvw = target.shape[1]
    groups = NX * NY
    own_rows = kvw // groups
    side = cols // 2
    capacity = 2 * rows // groups
    g, t = lax.axis_index("grp"), lax.axis_index("tp")
    z, core = t // CORES, t % CORES
    y, x = g // NX, g % NX
    other = 1 - core

    def along_z(k):
        return (g, ((z + k) % NZ) * CORES + core)

    def along_x(k):
        return (y * NX + (x + k) % NX, t)

    def along_y(k):
        return (((y + k) % NY) * NX + x, t)

    up, down, far = along_z(1), along_z(NZ - 1), along_z(2)
    sibling = (g, z * CORES + other)

    def pred_to(j):
        turn = z + x if j == 0 else 2 * NY - z - x
        return ((y + turn) % NY) * NX + 2 * core + j, g // 2

    def pred_from(j):
        source = 2 * t + j
        source_y, source_x = source // NX, source % NX
        odd = x % 2
        turn = (y - source_y + NY) * (1 - odd) + (source_y - y + NY) * odd
        return source, ((turn - source_x + 2 * NZ) % NZ) * CORES + x // 2

    def is_self(device):
        return jnp.logical_and(device[0] == g, device[1] == t)

    sends = []

    def copy_to(src, dst, send_sem, recv_sem, device):
        copy = pltpu.make_async_remote_copy(
            src_ref=src,
            dst_ref=dst,
            send_sem=send_sem,
            recv_sem=recv_sem,
            device_id=device,
            device_id_type=MESH,
        )
        copy.start()
        sends.append(copy)

    def wait_for(dst, send_sem, recv_sem, device):
        pltpu.make_async_remote_copy(
            src_ref=dst,
            dst_ref=dst,
            send_sem=send_sem,
            recv_sem=recv_sem,
            device_id=device,
            device_id_type=MESH,
        ).wait_recv()

    def place(which, cc):
        return pl.ds(pl.multiple_of((which * CORES + cc) * width, width), width)

    def block(which, cc, start, size):
        return a_all.at[pl.ds(start, size), place(which, cc)]

    loads = [
        pltpu.make_async_copy(master, mst_own, load_sem.at[0]),
        pltpu.make_async_copy(attn, block(OWN, core, 0, rows), load_sem.at[1]),
        pltpu.make_async_copy(residual, res_own, load_sem.at[2]),
        pltpu.make_async_copy(target, tgt_own, load_sem.at[3]),
    ]
    for which, step in ((OWN, 0), (UP, 1), (DOWN, NZ - 1), (FAR, 2)):
        for cc in range(CORES):
            first = ((z + step) % NZ * CORES + cc) * width
            loads.append(
                pltpu.make_async_copy(
                    o_proj.at[pl.ds(pl.multiple_of(first, width), width)],
                    w_own.at[place(which, cc)],
                    load_sem.at[4 + which * CORES + cc],
                )
            )
    for load in loads:
        load.start()

    barrier = pltpu.get_barrier_semaphore()

    def greet(device):
        pl.semaphore_signal(barrier, inc=1, device_id=device, device_id_type=MESH)

    for k in range(1, NZ):
        greet(along_z(k))
        greet(along_x(k))
        greet(along_y(k))
    greet(sibling)
    expected = jnp.int32(3 * (NZ - 1) + 1)
    for j in range(2):

        @pl.when(jnp.logical_not(is_self(pred_from(j))))
        def _():
            greet(pred_from(j))

        expected = expected + 1 - is_self(pred_to(j)).astype(jnp.int32)
    pl.semaphore_wait(barrier, expected)

    def send_own(i):
        start, size = STARTS[i], SIZES[i]
        src = attn.at[pl.ds(start, size)]
        copy_to(src, block(DOWN, core, start, size), ag_send.at[i, 0], ag_recv.at[i, 0], up)
        copy_to(src, block(UP, core, start, size), ag_send.at[i, 1], ag_recv.at[i, 1], down)
        copy_to(src, block(OWN, core, start, size), ag_send.at[i, 2], ag_recv.at[i, 2], sibling)

    send_own(0)
    send_own(1)

    def mst_rows(first, count):
        return mst_all.at[pl.ds(pl.multiple_of(first * own_rows, own_rows), count * own_rows)]

    loads[0].wait()
    mst_rows(g, 1)[...] = mst_own[...].astype(BF16)
    for k in range(1, NX):
        copy_to(mst_rows(g, 1), mst_rows(g, 1), m_send.at[0, k], m_recv.at[0, k], along_x(k))

    for n in range(rows // TILE):
        here = pl.ds(n * TILE, TILE)
        kinds = lax.broadcasted_iota(jnp.int32, (groups, rows), 0)
        onehot = (kinds == dest[...]).astype(F32).astype(BF16)
        earlier_rows = lax.broadcasted_iota(jnp.int32, (rows, TILE), 0)
        these_rows = lax.broadcasted_iota(jnp.int32, (rows, TILE), 1) + n * TILE
        before = (earlier_rows < these_rows).astype(F32).astype(BF16)
        earlier = jnp.dot(onehot, before, preferred_element_type=F32)
        dest_here = dest[:, here]
        mine = lax.broadcasted_iota(jnp.int32, (groups, TILE), 0) == dest_here
        rank = jnp.sum(jnp.where(mine, earlier, 0.0), axis=0, keepdims=True)
        spot[:, here] = dest_here * capacity + rank.astype(jnp.int32)

    requests = accept.shape[1]
    for n in range(rows // TILE):
        here = pl.ds(n * TILE, TILE)
        row = lax.broadcasted_iota(jnp.int32, (TILE, requests), 0) + n * TILE
        request = lax.broadcasted_iota(jnp.int32, (TILE, requests), 1)
        taken = jnp.sum(
            jnp.where(row // SPEC == request, accept[...], 0).astype(F32), axis=1, keepdims=True
        )
        order = (lax.broadcasted_iota(jnp.int32, (TILE, LANES), 0) % SPEC).astype(F32)
        live[here, :] = jnp.where(order < taken, 1.0, 0.0)

    for k in range(1, NX):
        source = along_x(NX - k)
        wait_for(mst_rows(source[0], 1), m_send.at[0, k], m_recv.at[0, k], source)
    for k in range(1, NY):
        src = mst_rows(y * NX, NX)
        copy_to(src, src, m_send.at[1, k], m_recv.at[1, k], along_y(k))

    def pass_on(i):
        start, size = STARTS[i], SIZES[i]
        part_size = size // 2
        src = block(DOWN, core, start, size)
        wait_for(src, ag_send.at[i, 0], ag_recv.at[i, 0], down)
        copy_to(
            block(DOWN, core, start, part_size),
            block(FAR, core, start, part_size),
            ag_send.at[i, 3],
            ag_recv.at[i, 3],
            up,
        )
        copy_to(src, src, ag_send.at[i, 4], ag_recv.at[i, 4], sibling)
        src = block(UP, core, start, size)
        wait_for(src, ag_send.at[i, 1], ag_recv.at[i, 1], up)
        copy_to(
            block(UP, core, start + part_size, part_size),
            block(FAR, core, start + part_size, part_size),
            ag_send.at[i, 5],
            ag_recv.at[i, 5],
            down,
        )
        copy_to(src, src, ag_send.at[i, 6], ag_recv.at[i, 6], sibling)
        if i + 2 < CHUNKS:
            send_own(i + 2)

    def pass_far(i):
        start, size = STARTS[i], SIZES[i]
        part_size = size // 2
        wait_for(
            block(FAR, core, start, part_size), ag_send.at[i, 3], ag_recv.at[i, 3], down
        )
        wait_for(
            block(FAR, core, start + part_size, part_size), ag_send.at[i, 5], ag_recv.at[i, 5], up
        )
        src = block(FAR, core, start, size)
        copy_to(src, src, ag_send.at[i, 7], ag_recv.at[i, 7], sibling)

    depth = FAR * CORES * width

    def multiply_near(i):
        start, size = STARTS[i], SIZES[i]
        here = pl.ds(start, size)
        for which, sem in ((OWN, 2), (DOWN, 4), (UP, 6)):
            wait_for(block(which, other, start, size), ag_send.at[i, sem], ag_recv.at[i, sem], sibling)
        if i == 0:
            for load in loads[1:]:
                load.wait()

        def columns(n, carry):
            there = pl.ds(pl.multiple_of(n * TILE, TILE), TILE)
            near[i % 2, :size, there] = jnp.dot(
                a_all[here, :depth], w_own[:depth, there], preferred_element_type=F32
            )
            return carry

        lax.fori_loop(0, cols // TILE, columns, 0, unroll=True)

    def multiply_far(i):
        start, size = STARTS[i], SIZES[i]
        here = pl.ds(start, size)
        wait_for(block(FAR, other, start, size), ag_send.at[i, 7], ag_recv.at[i, 7], sibling)

        def columns(n, squares):
            there = pl.ds(pl.multiple_of(n * TILE, TILE), TILE)
            hidden = near[i % 2, :size, there] + jnp.dot(
                a_all[here, depth:], w_own[depth:, there], preferred_element_type=F32
            )
            hidden = hidden + res_own[here, there].astype(F32)
            u_all[here, there] = (hidden * gain[:, there]).astype(BF16)
            squared = hidden * hidden
            return squares + squared[:, :LANES] + squared[:, LANES:]

        squares = lax.fori_loop(0, cols // TILE, columns, jnp.zeros((size, LANES), F32), unroll=True)
        total = jnp.sum(squares.T, axis=0, keepdims=True)
        sq_out[i, :, :size] = jnp.broadcast_to(total, (8, size))
        copy_to(sq_out.at[i], sq_pair.at[i], sq_send.at[i, 0], sq_recv.at[i, 0], sibling)
        if i == 0:
            for k in range(1, NY):
                source = (y + NY - k) % NY
                wait_for(
                    mst_rows(source * NX, NX), m_send.at[1, k], m_recv.at[1, k], along_y(NY - k)
                )
        part[here, :] = lax.dot_general(
            u_all[here, :],
            mst_all[...],
            (((1,), (1,)), ((), ())),
            preferred_element_type=F32,
        ).astype(BF16)
        half = size // CORES
        src = part.at[pl.ds(pl.multiple_of(start + other * half, half), half)]
        dst = pair_in.at[pl.ds(start // CORES, half)]
        copy_to(src, dst, vs_send.at[i, 0], vs_recv.at[i, 0], sibling)

    def add_pair(i):
        start, size = STARTS[i], SIZES[i]
        half = size // CORES
        sub = half // NZ
        first = start // CORES
        wait_for(sq_pair.at[i], sq_send.at[i, 0], sq_recv.at[i, 0], sibling)
        sq_sum[i] = sq_out[i] + sq_pair[i]
        for k in (2, 1, 3):
            copy_to(sq_sum.at[i], sq_z.at[i, k], sq_send.at[i, k], sq_recv.at[i, k], along_z(k))
        here = pl.ds(first, half)
        wait_for(pair_in.at[here], vs_send.at[i, 0], vs_recv.at[i, 0], sibling)
        mine = pl.ds(pl.multiple_of(start + core * half, half), half)
        pair_sum[here, :] = (part[mine, :].astype(F32) + pair_in[here, :].astype(F32)).astype(BF16)
        for k in (2, 1, 3):
            src = pair_sum.at[pl.ds(pl.multiple_of(first + (z + k) % NZ * sub, sub), sub)]
            dst = z_in.at[k, pl.ds(start // (CORES * NZ), sub)]
            copy_to(src, dst, vs_send.at[i, k], vs_recv.at[i, k], along_z(k))

    def own_part(i, zz):
        sub = SIZES[i] // (CORES * NZ)
        return pl.ds(pl.multiple_of(STARTS[i] + (core * NZ + zz) * sub, sub), sub)

    def finish_values(i):
        start, size = STARTS[i], SIZES[i]
        sub = size // (CORES * NZ)
        total = sq_sum[i]
        for k in (2, 1, 3):
            wait_for(sq_z.at[i, k], sq_send.at[i, k], sq_recv.at[i, k], along_z(NZ - k))
            total = total + sq_z[i, k]
        scale = lax.rsqrt(total[:1, :size] / D + norm_eps)
        scales[pl.ds(start, size), :] = jnp.broadcast_to(scale, (LANES, size)).T
        mine = pl.ds(pl.multiple_of(start // CORES + z * sub, sub), sub)
        there = pl.ds(start // (CORES * NZ), sub)
        values = pair_sum[mine, :].astype(F32)
        for k in (2, 1, 3):
            wait_for(z_in.at[k, there], vs_send.at[i, k], vs_recv.at[i, k], along_z(NZ - k))
            values = values + z_in[k, there, :].astype(F32)
        here = own_part(i, z)
        val_all[here, :] = (values * scales[here, :1]).astype(BF16)
        src = val_all.at[here]
        for k in (2, 1, 3):
            copy_to(src, src, vs_send.at[i, 3 + k], vs_recv.at[i, 3 + k], along_z(k))

    def pass_values(i):
        half = SIZES[i] // CORES
        for k in (2, 1, 3):
            dst = val_all.at[own_part(i, (z + NZ - k) % NZ)]
            wait_for(dst, vs_send.at[i, 3 + k], vs_recv.at[i, 3 + k], along_z(NZ - k))
        src = val_all.at[pl.ds(pl.multiple_of(STARTS[i] + core * half, half), half)]
        copy_to(src, src, vs_send.at[i, 7], vs_recv.at[i, 7], sibling)

    def send_first():
        for k in range(1, NX):
            src, dst = g_one_out.at[(x + k) % NX], g_one_in.at[k]
            copy_to(src, dst, g_send.at[0, k], g_recv.at[0, k], along_x(k))

    def send_second():
        for k in range(1, NY):
            src, dst = g_two_out.at[(y + k) % NY], g_two_in.at[k]
            copy_to(src, dst, g_send.at[1, k], g_recv.at[1, k], along_y(k))

    def add_gradient(i):
        start, size = STARTS[i], SIZES[i]
        half = size // CORES
        dst = val_all.at[pl.ds(pl.multiple_of(start + other * half, half), half)]
        wait_for(dst, vs_send.at[i, 7], vs_recv.at[i, 7], sibling)
        here = pl.ds(start, size)
        weight = live[here, :1] * scales[here, :1]
        errors = weight * (val_all[here, :].astype(F32) - tgt_own[here, :].astype(F32))
        errors = errors.astype(BF16)
        for part_of, send in ((0, send_first), (1, send_second)):
            there = pl.ds(part_of * side, side)
            product = lax.dot_general(
                errors, u_all[here, there], (((0,), (0,)), ((), ())), preferred_element_type=F32
            )
            if i > 0:
                product = product + g_sum[:, there]
            g_sum[:, there] = product
            if i == CHUNKS - 1:
                for yy in range(NY):
                    for xx in range(NX):
                        first = (yy * NX + xx) * own_rows
                        piece = product[first : first + own_rows].astype(BF16)
                        if part_of == 0:
                            g_one_out[xx, yy] = piece
                        else:
                            g_two_out[yy, xx] = piece
                send()

    for it in range(CHUNKS + 5):
        for stage, lag in (
            (pass_on, 0),
            (add_pair, 2),
            (finish_values, 3),
            (pass_values, 4),
            (multiply_near, 0),
            (pass_far, 1),
            (multiply_far, 1),
            (add_gradient, 5),
        ):
            if 0 <= it - lag < CHUNKS:
                stage(it - lag)

    slot = lax.broadcasted_iota(jnp.int32, (capacity, rows), 0)
    for j in range(2):
        pick = (slot + pred_to(j)[0] * capacity == spot[...]).astype(F32).astype(BF16)
        p_out[j] = jnp.dot(pick, val_all[...], preferred_element_type=F32).astype(BF16)

    def pred_copy(j):
        return pltpu.make_async_remote_copy(
            src_ref=p_out.at[j],
            dst_ref=pred.at[pl.ds(pl.multiple_of((g % 2) * capacity, capacity), capacity)],
            send_sem=p_send.at[j],
            recv_sem=p_recv.at[g % 2],
            device_id=pred_to(j),
            device_id_type=MESH,
        )

    def pred_local(j):
        return pltpu.make_async_copy(
            p_out.at[j],
            pred.at[pl.ds(pl.multiple_of((g % 2) * capacity, capacity), capacity)],
            p_send.at[j],
        )

    for j in range(2):

        @pl.when(is_self(pred_to(j)))
        def _():
            pred_local(j).start()

        @pl.when(jnp.logical_not(is_self(pred_to(j))))
        def _():
            pred_copy(j).start()

    early = len(sends) - NX - NY + 2
    for copy in sends[:early]:
        copy.wait_send()
    del sends[:early]

    for k in range(1, NX):
        wait_for(g_one_in.at[k], g_send.at[0, k], g_recv.at[0, k], along_x(NX - k))
    for yy in range(NY):
        mine = pl.ds(pl.multiple_of((yy * NX + x) * own_rows, own_rows), own_rows)
        total = g_sum[mine, :side]
        for k in range(1, NX):
            total = total + g_one_in[k, yy].astype(F32)
        h_one[yy] = total
        h_one_out[yy] = total.astype(BF16)
    for k in range(1, NY):
        src, dst = h_one_out.at[(y + k) % NY], h_one_in.at[k]
        copy_to(src, dst, g_send.at[2, k], g_recv.at[2, k], along_y(k))
    for k in range(1, NY):
        wait_for(g_two_in.at[k], g_send.at[1, k], g_recv.at[1, k], along_y(NY - k))
    for xx in range(NX):
        mine = pl.ds(pl.multiple_of((y * NX + xx) * own_rows, own_rows), own_rows)
        total = g_sum[mine, side:]
        for k in range(1, NY):
            total = total + g_two_in[k, xx].astype(F32)
        h_two[xx] = total
        h_two_out[xx] = total.astype(BF16)
    for k in range(1, NX):
        src, dst = h_two_out.at[(x + k) % NX], h_two_in.at[k]
        copy_to(src, dst, g_send.at[3, k], g_recv.at[3, k], along_x(k))
    norm = 1.0 / math.sqrt(rows * groups)
    total = h_one[y]
    for k in range(1, NY):
        wait_for(h_one_in.at[k], g_send.at[2, k], g_recv.at[2, k], along_y(NY - k))
        total = total + h_one_in[k].astype(F32)
    grad[:, :side] = total * norm
    total = h_two[x]
    for k in range(1, NX):
        wait_for(h_two_in.at[k], g_send.at[3, k], g_recv.at[3, k], along_x(NX - k))
        total = total + h_two_in[k].astype(F32)
    grad[:, side:] = total * norm

    for j in range(2):

        @pl.when(is_self(pred_to(j)))
        def _():
            pred_local(j).wait()

        @pl.when(jnp.logical_not(is_self(pred_to(j))))
        def _():
            pred_copy(j).wait_send()

        @pl.when(jnp.logical_not(is_self(pred_from(j))))
        def _():
            dst = pred.at[pl.ds(j * capacity, capacity)]
            wait_for(dst, p_send.at[j], p_recv.at[j], pred_from(j))

    for copy in sends:
        copy.wait_send()


def local(
    attn_out,
    o_proj,
    residual,
    norm_gain,
    dest_group,
    accept_count,
    target_values,
    master,
    moment_one,
    moment_two,
):
    groups = lax.axis_size("grp")
    rows, width = attn_out.shape
    depth, cols = o_proj.shape
    kvw = target_values.shape[1]
    own_rows = master.shape[0]
    capacity = 2 * rows // groups
    side = cols // 2
    largest = max(SIZES)
    any_spec = pl.BlockSpec(memory_space=pl.ANY)
    vmem_spec = pl.BlockSpec(memory_space=pltpu.VMEM)
    vmem = pltpu.VMEM
    dma = pltpu.SemaphoreType.DMA
    pred, grad = pl.pallas_call(
        kernel,
        out_shape=(
            jax.ShapeDtypeStruct((2 * capacity, kvw), BF16),
            jax.ShapeDtypeStruct((own_rows, cols), F32),
        ),
        in_specs=[any_spec, any_spec, any_spec, vmem_spec, vmem_spec, vmem_spec, any_spec, any_spec],
        out_specs=(any_spec, vmem_spec),
        scratch_shapes=[
            vmem((rows, depth), BF16),
            vmem((depth, cols), BF16),
            vmem((rows, cols), BF16),
            vmem((rows, kvw), BF16),
            vmem((own_rows, cols), F32),
            vmem((kvw, cols), BF16),
            vmem((rows, cols), BF16),
            vmem((2, largest, cols), F32),
            vmem((rows, kvw), BF16),
            vmem((rows // CORES, kvw), BF16),
            vmem((rows // CORES, kvw), BF16),
            vmem((NZ, rows // (CORES * NZ), kvw), BF16),
            vmem((rows, kvw), BF16),
            vmem((CHUNKS, 8, largest), F32),
            vmem((CHUNKS, 8, largest), F32),
            vmem((CHUNKS, 8, largest), F32),
            vmem((CHUNKS, NZ, 8, largest), F32),
            vmem((rows, LANES), F32),
            vmem((rows, LANES), F32),
            vmem((kvw, cols), F32),
            vmem((NX, NY, own_rows, side), BF16),
            vmem((NY, NX, own_rows, side), BF16),
            vmem((NX, NY, own_rows, side), BF16),
            vmem((NY, NX, own_rows, side), BF16),
            vmem((NY, own_rows, side), F32),
            vmem((NX, own_rows, side), F32),
            vmem((NY, own_rows, side), BF16),
            vmem((NX, own_rows, side), BF16),
            vmem((NY, own_rows, side), BF16),
            vmem((NX, own_rows, side), BF16),
            vmem((2, capacity, kvw), BF16),
            vmem((1, rows), jnp.int32),
            dma((12,)),
            dma((CHUNKS, 8)),
            dma((CHUNKS, 8)),
            dma((CHUNKS, 8)),
            dma((CHUNKS, 8)),
            dma((CHUNKS, NZ)),
            dma((CHUNKS, NZ)),
            dma((2, NX)),
            dma((2, NX)),
            dma((4, NX)),
            dma((4, NX)),
            dma((2,)),
            dma((2,)),
        ],
        compiler_params=pltpu.CompilerParams(
            collective_id=0, has_side_effects=True, vmem_limit_bytes=56 * 2**20
        ),
        cost_estimate=pl.CostEstimate(
            flops=2 * rows * cols * (depth + 2 * kvw),
            bytes_accessed=2 * (depth * cols + rows * (cols + width + kvw)),
            transcendentals=0,
        ),
        name="step",
    )(
        attn_out,
        o_proj,
        residual,
        norm_gain.reshape(1, cols),
        dest_group.reshape(1, rows),
        accept_count.reshape(1, rows // SPEC),
        target_values,
        master,
    )
    own = jax.ShapeDtypeStruct((own_rows, cols), F32)
    return pl.pallas_call(
        finish_kernel,
        out_shape=(jax.ShapeDtypeStruct((2 * capacity, kvw), BF16), own, own, own),
        in_specs=[vmem_spec] * 5,
        out_specs=(vmem_spec,) * 4,
        cost_estimate=pl.CostEstimate(
            flops=16 * own_rows * cols, bytes_accessed=28 * own_rows * cols, transcendentals=0
        ),
        name="finish",
    )(pred, grad, master, moment_one, moment_two)


def solution(mesh):
    in_specs = (
        P("grp", "tp"),
        P(None, "tp"),
        P("grp", "tp"),
        P("tp"),
        P("grp", None),
        P("grp"),
        P("grp", None),
        P("grp", "tp"),
        P("grp", "tp"),
        P("grp", "tp"),
    )
    out_specs = (P(("grp", "tp"), None), P("grp", "tp"), P("grp", "tp"), P("grp", "tp"))
    return jax.shard_map(local, mesh=mesh, in_specs=in_specs, out_specs=out_specs, check_vma=False)
```
